32 devices in a mesh: ex: 8 (over z, core), pb: 4 (over y, x).
Axes of the slice: x: 2, y: 2, z: 4, core: 2. Of those that a mesh axis runs over, the one named last changes fastest.
Arguments:
- train_sketch: bfloat16 [6144, 8192], P(('ex', 'pb')), may hold values from -6 to 6
- query_sketch: bfloat16 [768, 8192], P('pb'), may hold values from -0.0625 to 0.0625
- residual: float32 [6144], P(('ex', 'pb')), may hold values from 0.05 to 1
- example_source: int32 [6144], P(('ex', 'pb')), may hold values from 0 to 8191, as said below
- source_place: int32 [8192], replicated, may hold values from 0 to 8191, as said below
Outputs:
- source_scores: float32 [8192, 768], P(('ex', 'pb'))
The draws below stay inside these ranges and needn't reach their ends.
Inputs may be any that keep to these rules, and one draw needn't show every extreme that they name: source_place names each row 0 to 8191 once. `example_source`: of the 192 examples of one device, at most 48 have sources whose table row lies with any one owner (row // 1024); one owner receives exactly 48 from every device. Of them, at most 12 have table rows in any one share of that owner (row % 1024 // (1024 / 4)); in every draw some share of one owner receives exactly 12 from every device.
All inputs are finite; a program needn't handle non-finite values.
Results may differ from the reference program's by a relative error of at most 0.0029.
Values may be sent and summed in bfloat16 or wider, within the bound.
No kernel may reach another device: no remote copies, remote signals or barrier semaphores. Data moves between devices by JAX's collectives and lax.ppermute only.
A program may use at most 64 MiB of HBM per device.

```python
import jax
import jax.numpy as jnp

K = 8192
Q = 768
ROWS = 192
SRC_DEV = 1024
CAP = 48
EXAMPLES = 6144
SOURCES = 8192
N_EX = 8
N_PB = 4


def swap_entry(table, value, position):
    found = jnp.argmax((table == value).astype(jnp.int32)).astype(jnp.int32)
    there = table[position]
    table = table.at[found].set(there)
    return table.at[position].set(value)


def joint_tables(key):
    base = jax.random.fold_in(key, 11)
    key_place, key_hot, key_perm, key_rows, key_slot = jax.random.split(base, 5)
    blocks = N_EX * N_PB
    share_width = SRC_DEV // N_PB
    hottest = jax.random.randint(key_hot, (), 0, N_EX).astype(jnp.int32)
    inverse = jax.random.permutation(key_place, SOURCES).astype(jnp.int32)
    inverse = swap_entry(inverse, jnp.int32(0), hottest * SRC_DEV)
    inverse = swap_entry(inverse, jnp.int32(SOURCES - 1), hottest * SRC_DEV + 2 * share_width - 1)
    placed = jnp.zeros((SOURCES,), jnp.int32).at[inverse].set(jnp.arange(SOURCES, dtype=jnp.int32))
    others = jax.vmap(lambda k: jax.random.permutation(k, N_EX - 1))(jax.random.split(key_perm, blocks)).astype(jnp.int32)
    column = jnp.arange(ROWS, dtype=jnp.int32)
    index_other = (column - CAP) % (N_EX - 1)
    picked = others[:, index_other]
    picked = jnp.where(picked >= hottest, picked + 1, picked)
    owner_id = jnp.where(column[None, :] < CAP, hottest, picked).astype(jnp.int32)
    rank_owner = jnp.where(column < CAP, column, (column - CAP) // (N_EX - 1)).astype(jnp.int32)
    share_no = (rank_owner % N_PB).astype(jnp.int32)
    within = jax.random.randint(key_slot, (blocks, ROWS), 0, share_width).astype(jnp.int32)
    block_no = jnp.arange(blocks, dtype=jnp.int32)[:, None]
    within = jnp.where((block_no == 0) & (column[None, :] < 2), column[None, :] * (share_width - 1), within).astype(jnp.int32)
    slot_id = (share_no[None, :] * share_width + within).astype(jnp.int32)
    orders = jax.vmap(lambda k: jax.random.permutation(k, ROWS))(jax.random.split(key_rows, blocks)).astype(jnp.int32)
    owner_id = jnp.take_along_axis(owner_id, orders, axis=1)
    slot_id = jnp.take_along_axis(slot_id, orders, axis=1)
    source_ids = inverse[owner_id * SRC_DEV + slot_id].reshape(-1)
    return (placed, source_ids)


def draw_source_place(key, part):
    return joint_tables(key)[0]


def draw_example_source(key, part):
    return joint_tables(key)[1]


def steps_of(rng, shape, cuts, low, top_value):
    factor_of = 1.0
    for dim, blocks in cuts:
        draws = jax.random.uniform(jax.random.fold_in(jax.random.fold_in(rng, 6), dim), (blocks,), jnp.float32, low / len(cuts), top_value / len(cuts))
        factor_of = factor_of * jnp.repeat(jnp.exp(draws), shape[dim] // blocks).reshape((-1,) + (1,) * (len(shape) - 1 - dim))
    return factor_of


def scatter_about(own_key, dims, spread, limit, shards=(), kind=jnp.bfloat16):
    drawn = jax.random.normal(own_key, dims, jnp.float32) * spread
    if len(shards) > 0:
        drawn = steps_of(own_key, dims, shards, -0.22, 0.18) * drawn
    return jnp.clip(drawn, min=-limit, max=limit).astype(kind)


def setup_inputs(seed: int = 0) -> dict:
    key_of = jax.random.split(jax.random.key(seed), 6)
    train_sketch = scatter_about(key_of[0], (EXAMPLES, K), 1.0, 6.0, ((0, 32),))
    query_sketch = scatter_about(key_of[1], (Q, K), K ** -0.5, 0.0625, ((0, 4),))
    residual = jnp.clip(0.05 + 0.95 * jax.random.uniform(key_of[2], (EXAMPLES,), jnp.float32) ** steps_of(key_of[2], (EXAMPLES,), ((0, 32),), -0.2, 0.2), 0.05, 1.0)
    example_source = draw_example_source(jax.random.fold_in(key_of[5], 71), 0)
    source_place = draw_source_place(jax.random.fold_in(key_of[5], 71), 0)
    return {"train_sketch": train_sketch, "query_sketch": query_sketch, "residual": residual, "example_source": example_source, "source_place": source_place}


def reference(train_sketch, query_sketch, residual, example_source, source_place):
    scores = jnp.dot(train_sketch, query_sketch.T, preferred_element_type=jnp.float32)
    weighted = (scores * residual[:, None]).astype(jnp.bfloat16)
    placed = source_place[example_source]
    return jax.ops.segment_sum(weighted.astype(jnp.float32), placed, num_segments=SOURCES)
```

```python
import functools
import math

import jax
import jax.numpy as jnp
from jax import lax
from jax.experimental import pallas as pl
from jax.experimental.pallas import tpu as pltpu
from jax.sharding import PartitionSpec as P

BOTH = ("ex", "pb")
NT = (((1,), (1,)), ((), ()))


def moved(value, axis, target):
    count = lax.axis_size(axis)
    return lax.ppermute(value, axis, [(i, target(i)) for i in range(count)])


def partial_kernel(count, own_ref, other_ref, *refs):
    pieces, (own_out, other_out) = refs[:count], refs[count:]
    queries = jnp.concatenate([piece[...] for piece in pieces], axis=0)

    @pl.when(pl.program_id(0) == 0)
    def _():
        own_out[...] = jnp.zeros_like(own_out)
        other_out[...] = jnp.zeros_like(other_out)

    other_out[...] += lax.dot_general(other_ref[...], queries, NT, preferred_element_type=jnp.float32)
    own_out[...] += lax.dot_general(own_ref[...], queries, NT, preferred_element_type=jnp.float32)


def partials(own, other, pieces):
    rows, depth = own.shape
    width = sum(piece.shape[0] for piece in pieces)
    step = math.gcd(depth, 1024)
    chunk = lambda height: pl.BlockSpec((height, step), lambda k: (0, k))
    whole = pl.BlockSpec((rows, width), lambda k: (0, 0))
    return pl.pallas_call(
        functools.partial(partial_kernel, len(pieces)),
        grid=(depth // step,),
        in_specs=[chunk(rows), chunk(rows)] + [chunk(piece.shape[0]) for piece in pieces],
        out_specs=[whole, whole],
        out_shape=[jax.ShapeDtypeStruct((rows, width), jnp.float32)] * 2,
        compiler_params=pltpu.CompilerParams(vmem_limit_bytes=40 << 20),
        cost_estimate=pl.CostEstimate(
            flops=4 * rows * width * depth, bytes_accessed=2 * depth * (2 * rows + width), transcendentals=0
        ),
    )(own, other, *pieces)


def one_hot(hits):
    return jnp.where(hits, 1.0, 0.0).astype(jnp.bfloat16)


def pick(select, values):
    return jnp.dot(select, values, preferred_element_type=jnp.float32)


def packed_kernel(full, own_a, got_a, own_b, got_b, residual_ref, column_ref, target_ref, out_ref):
    scale = residual_ref[...]
    weighted = jnp.concatenate(
        [
            ((own_a[...] + got_a[...]) * scale).astype(jnp.bfloat16),
            ((own_b[...] + got_b[...]) * scale).astype(jnp.bfloat16),
        ],
        axis=1,
    )
    rows, width = weighted.shape
    order = one_hot(lax.broadcasted_iota(jnp.int32, (width, width), 1) == column_ref[...])
    ordered = pick(weighted, order).astype(jnp.bfloat16)
    height = out_ref.shape[0]
    at = 0
    for index in range(full // 8):
        row = lax.broadcasted_iota(jnp.int32, (height, rows), 0)
        select = one_hot(row == target_ref[index : index + 1, :])
        out_ref[:, at : at + width] = pick(select, ordered).astype(jnp.bfloat16)
        at += width
    if out_ref.shape[1] > at:
        half = width // 2
        index = full // 8
        row = lax.broadcasted_iota(jnp.int32, (height, rows), 0)
        left = one_hot(row == target_ref[index : index + 1, :])
        right = one_hot(row == target_ref[index + 1 : index + 2, :])
        both = pick(left, ordered[:, :half]) + pick(right, ordered[:, half:])
        out_ref[:, at:] = both.astype(jnp.bfloat16)


def table_kernel(full, got_ref, slot_ref, out_ref):
    height, width = out_ref.shape
    received = got_ref.shape[0]
    row = lax.broadcasted_iota(jnp.int32, (height, received), 0)
    total = None
    at = 0
    for index in range(full // 8):
        part = pick(one_hot(row == slot_ref[index : index + 1, :]), got_ref[:, at : at + width])
        total = part if total is None else total + part
        at += width
    if got_ref.shape[1] > at:
        half = width // 2
        index = full // 8
        for side in range(2):
            part = pick(one_hot(row == slot_ref[index + side : index + side + 1, :]), got_ref[:, at:])
            span = slice(side * half, (side + 1) * half)
            out_ref[:, span] = part if total is None else total[:, span] + part
    else:
        out_ref[...] = total


def on_device(train, query, residual, example_source, source_place):
    rows, depth = train.shape
    block = query.shape[0]
    ex, pb = lax.axis_size("ex"), lax.axis_size("pb")
    me_ex, me_pb = lax.axis_index("ex"), lax.axis_index("pb")
    devices = ex * pb
    side = math.isqrt(pb)
    assert side * side == pb and ex % 4 == 0
    table_rows = source_place.shape[0] // devices
    core, layer = me_ex % 2, (me_ex // 2) % 2
    deep = depth // 2
    half = block // 2
    lent = half * 2 // 3 // 8 * 8

    along_x = lambda d: lambda i: i // side * side + (i + d) % side
    along_y = lambda d: lambda i: (i + d * side) % pb
    on_core = lambda i: i ^ 1
    on_z = lambda i: i ^ 2
    steps = range(1, side)

    first = layer * half
    second = half - first
    cut = lambda start, count: lax.dynamic_slice(query, (start, core * deep), (count, deep))
    front, back = cut(first, half), cut(second, half)
    x_one = [moved(front, "pb", along_x(d)) for d in steps]
    y_one = [moved(back, "pb", along_y(d)) for d in steps]
    x_rest = [moved(back[lent:], "pb", along_x(d)) for d in steps]
    y_rest = [moved(front[lent:], "pb", along_y(d)) for d in steps]
    other = moved(lax.dynamic_slice(train, (0, (1 - core) * deep), (rows, deep)), "ex", on_core)
    own = lax.dynamic_slice(train, (0, core * deep), (rows, deep))

    placed = jnp.take(source_place, example_source)
    placed_all = lax.all_gather(placed, BOTH, tiled=True).reshape(devices, rows)
    capacity = max(1, -(-2 * rows // devices))
    full, rest = capacity // 8 * 8, capacity % 8
    if rest > 4:
        full, rest = full + 8, 0
    goal = placed // table_rows
    before = jnp.arange(rows)[None, :] < jnp.arange(rows)[:, None]
    rank = jnp.sum((goal[:, None] == goal[None, :]) & before, axis=1).astype(jnp.int32)
    groups = [jnp.where(rank // 8 == index, goal * 8 + rank % 8, -1) for index in range(full // 8)]
    if rest:
        late = rank >= full
        groups += [jnp.where(late, goal * 8 + g * 4 + rank - full, -1) for g in range(2)]
    target = jnp.stack(groups)

    mine = placed_all // table_rows == me_ex * pb + me_pb
    rank_all = jnp.cumsum(mine.astype(jnp.int32), axis=1) - 1
    slot_all = placed_all % table_rows

    def slots(rank_wanted):
        hit = mine[:, None, :] & (rank_all[:, None, :] == rank_wanted[None, :, None])
        found = jnp.sum(jnp.where(hit, slot_all[:, None, :] + 1, 0), axis=2) - 1
        return found.reshape(devices * 8)

    eight = jnp.arange(8, dtype=jnp.int32)
    slot_groups = [slots(eight + 8 * index) for index in range(full // 8)]
    if rest:
        slot_groups += [slots(jnp.where(eight // 4 == g, full + eight % 4, rows)) for g in range(2)]
    slot = jnp.stack(slot_groups)

    early = [front, back] + x_one + y_one
    early_own, early_other = partials(own, other, early)
    early_got = moved(early_other, "ex", on_core)

    x_lent = moved(jnp.concatenate([v[:lent] for v in x_one], axis=0), "ex", on_z)
    y_lent = moved(jnp.concatenate([v[:lent] for v in y_one], axis=0), "ex", on_z)
    y_all = y_one[0] if side == 2 else jnp.concatenate(y_one, axis=0)
    x_all = x_one[0] if side == 2 else jnp.concatenate(x_one, axis=0)
    x_two = [moved(y_all, "pb", along_x(d)) for d in steps]
    y_two = [moved(x_all, "pb", along_y(d)) for d in steps]
    late_pieces = x_two + y_two + [x_lent, y_lent] + x_rest + y_rest
    late_own, late_other = partials(own, other, late_pieces)
    late_got = moved(late_other, "ex", on_core)

    my_x, my_y = me_pb % side, me_pb // side
    at = lambda dx, dy: ((my_y - dy) % side * side + (my_x - dx) % side) * block
    span = lambda start, count: start + jnp.arange(count, dtype=jnp.int32)
    columns = [span(at(0, 0) + first, half), span(at(0, 0) + second, half)]
    columns += [span(at(d, 0) + first, half) for d in steps]
    columns += [span(at(0, d) + second, half) for d in steps]
    for d in steps:
        columns += [span(at(d, up) + second, half) for up in steps]
    for up in steps:
        columns += [span(at(d, up) + first, half) for d in steps]
    columns += [span(at(d, 0) + second, lent) for d in steps]
    columns += [span(at(0, d) + first, lent) for d in steps]
    columns += [span(at(d, 0) + second + lent, half - lent) for d in steps]
    columns += [span(at(0, d) + first + lent, half - lent) for d in steps]
    column = jnp.concatenate(columns)[:, None]

    width = block * pb
    payload = full // 8 * width + (width // 2 if rest else 0)
    packed = pl.pallas_call(
        functools.partial(packed_kernel, full),
        out_shape=jax.ShapeDtypeStruct((devices * 8, payload), jnp.bfloat16),
        compiler_params=pltpu.CompilerParams(vmem_limit_bytes=48 << 20),
    )(early_own, early_got, late_own, late_got, residual[:, None], column, target)
    got = lax.all_to_all(packed.reshape(devices, 8, payload), BOTH, split_axis=0, concat_axis=0)
    return pl.pallas_call(
        functools.partial(table_kernel, full),
        out_shape=jax.ShapeDtypeStruct((table_rows, width), jnp.float32),
        compiler_params=pltpu.CompilerParams(vmem_limit_bytes=48 << 20),
    )(got.reshape(devices * 8, payload), slot)


def solution(mesh):
    return jax.shard_map(
        on_device,
        mesh=mesh,
        in_specs=(P(BOTH, None), P("pb", None), P(BOTH), P(BOTH), P()),
        out_specs=P(BOTH, None),
        check_vma=False,
    )
```

```python
import functools
import math

import jax
import jax.numpy as jnp
from jax import lax
from jax.experimental import pallas as pl
from jax.experimental.pallas import tpu as pltpu
from jax.sharding import PartitionSpec as P

BOTH = ("ex", "pb")
NT = (((1,), (1,)), ((), ()))


def moved(value, axis, target):
    count = lax.axis_size(axis)
    return lax.ppermute(value, axis, [(i, target(i)) for i in range(count)])


def partial_kernel(count, own_ref, other_ref, *refs):
    pieces, (own_out, other_out) = refs[:count], refs[count:]
    queries = jnp.concatenate([piece[...] for piece in pieces], axis=0)

    @pl.when(pl.program_id(0) == 0)
    def _():
        own_out[...] = jnp.zeros_like(own_out)
        other_out[...] = jnp.zeros_like(other_out)

    other_out[...] += lax.dot_general(other_ref[...], queries, NT, preferred_element_type=jnp.float32)
    own_out[...] += lax.dot_general(own_ref[...], queries, NT, preferred_element_type=jnp.float32)


def partials(own, other, pieces):
    rows, depth = own.shape
    width = sum(piece.shape[0] for piece in pieces)
    step = math.gcd(depth, 1024)
    chunk = lambda height: pl.BlockSpec((height, step), lambda k: (0, k))
    whole = pl.BlockSpec((rows, width), lambda k: (0, 0))
    return pl.pallas_call(
        functools.partial(partial_kernel, len(pieces)),
        grid=(depth // step,),
        in_specs=[chunk(rows), chunk(rows)] + [chunk(piece.shape[0]) for piece in pieces],
        out_specs=[whole, whole],
        out_shape=[jax.ShapeDtypeStruct((rows, width), jnp.float32)] * 2,
        compiler_params=pltpu.CompilerParams(vmem_limit_bytes=40 << 20),
        cost_estimate=pl.CostEstimate(
            flops=4 * rows * width * depth, bytes_accessed=2 * depth * (2 * rows + width), transcendentals=0
        ),
    )(own, other, *pieces)


def one_hot(hits):
    return jnp.where(hits, 1.0, 0.0).astype(jnp.bfloat16)


def pick(select, values):
    return jnp.dot(select, values, preferred_element_type=jnp.float32)


def packed_kernel(full, own_a, got_a, own_b, got_b, residual_ref, column_ref, target_ref, out_ref):
    scale = residual_ref[...]
    weighted = jnp.concatenate(
        [
            ((own_a[...] + got_a[...]) * scale).astype(jnp.bfloat16),
            ((own_b[...] + got_b[...]) * scale).astype(jnp.bfloat16),
        ],
        axis=1,
    )
    rows, width = weighted.shape
    order = one_hot(lax.broadcasted_iota(jnp.int32, (width, width), 1) == column_ref[...])
    ordered = pick(weighted, order).astype(jnp.bfloat16)
    height = out_ref.shape[0]
    at = 0
    for index in range(full // 8):
        row = lax.broadcasted_iota(jnp.int32, (height, rows), 0)
        select = one_hot(row == target_ref[index : index + 1, :])
        out_ref[:, at : at + width] = pick(select, ordered).astype(jnp.bfloat16)
        at += width
    if out_ref.shape[1] > at:
        half = width // 2
        index = full // 8
        row = lax.broadcasted_iota(jnp.int32, (height, rows), 0)
        left = one_hot(row == target_ref[index : index + 1, :])
        right = one_hot(row == target_ref[index + 1 : index + 2, :])
        both = pick(left, ordered[:, :half]) + pick(right, ordered[:, half:])
        out_ref[:, at:] = both.astype(jnp.bfloat16)


def table_kernel(full, got_ref, slot_ref, out_ref):
    height, width = out_ref.shape
    received = got_ref.shape[0]
    row = lax.broadcasted_iota(jnp.int32, (height, received), 0)
    total = None
    at = 0
    for index in range(full // 8):
        part = pick(one_hot(row == slot_ref[index : index + 1, :]), got_ref[:, at : at + width])
        total = part if total is None else total + part
        at += width
    if got_ref.shape[1] > at:
        half = width // 2
        index = full // 8
        for side in range(2):
            part = pick(one_hot(row == slot_ref[index + side : index + side + 1, :]), got_ref[:, at:])
            span = slice(side * half, (side + 1) * half)
            out_ref[:, span] = part if total is None else total[:, span] + part
    else:
        out_ref[...] = total


def on_device(train, query, residual, example_source, source_place):
    rows, depth = train.shape
    block = query.shape[0]
    ex, pb = lax.axis_size("ex"), lax.axis_size("pb")
    me_ex, me_pb = lax.axis_index("ex"), lax.axis_index("pb")
    devices = ex * pb
    side = math.isqrt(pb)
    assert side * side == pb and ex % 4 == 0
    table_rows = source_place.shape[0] // devices
    core, layer = me_ex % 2, (me_ex // 2) % 2
    deep = depth // 2
    half = block // 2
    lent = half * 2 // 3 // 8 * 8

    along_x = lambda d: lambda i: i // side * side + (i + d) % side
    along_y = lambda d: lambda i: (i + d * side) % pb
    on_core = lambda i: i ^ 1
    on_z = lambda i: i ^ 2
    steps = range(1, side)

    first = layer * half
    second = half - first
    cut = lambda start, count: lax.dynamic_slice(query, (start, core * deep), (count, deep))
    front, back = cut(first, half), cut(second, half)
    x_one = [moved(front, "pb", along_x(d)) for d in steps]
    y_one = [moved(back, "pb", along_y(d)) for d in steps]
    x_rest = [moved(back[lent:], "pb", along_x(d)) for d in steps]
    y_rest = [moved(front[lent:], "pb", along_y(d)) for d in steps]
    other = moved(lax.dynamic_slice(train, (0, (1 - core) * deep), (rows, deep)), "ex", on_core)
    own = lax.dynamic_slice(train, (0, core * deep), (rows, deep))

    placed = jnp.take(source_place, example_source)
    capacity = max(1, -(-2 * rows // devices))
    full, rest = capacity // 8 * 8, capacity % 8
    if rest > 4:
        full, rest = full + 8, 0
    goal = placed // table_rows
    before = jnp.arange(rows)[None, :] < jnp.arange(rows)[:, None]
    rank = jnp.sum((goal[:, None] == goal[None, :]) & before, axis=1).astype(jnp.int32)
    groups = [jnp.where(rank // 8 == index, goal * 8 + rank % 8, -1) for index in range(full // 8)]
    if rest:
        late = rank >= full
        groups += [jnp.where(late, goal * 8 + g * 4 + rank - full, -1) for g in range(2)]
    target = jnp.stack(groups)

    lanes = -(-capacity // 128) * 128
    there = goal[None, None, :] == jnp.arange(devices, dtype=jnp.int32)[:, None, None]
    hit = there & (rank[None, None, :] == jnp.arange(capacity, dtype=jnp.int32)[None, :, None])
    wanted = jnp.sum(jnp.where(hit, (placed % table_rows + 1)[None, None, :], 0), axis=2) - 1
    wanted = jnp.pad(wanted, ((0, 0), (0, lanes - capacity)), constant_values=-1)
    slot_all = lax.all_to_all(wanted.reshape(devices, 1, lanes), BOTH, split_axis=0, concat_axis=0)
    slot_all = jnp.pad(slot_all[:, 0, :capacity], ((0, 0), (0, 8)), constant_values=-1)

    slot_groups = [slot_all[:, 8 * index : 8 * index + 8] for index in range(full // 8)]
    if rest:
        tail = jnp.where(jnp.arange(4) < rest, slot_all[:, full : full + 4], -1)
        none = jnp.full_like(tail, -1)
        slot_groups += [jnp.concatenate(pair, axis=1) for pair in ((tail, none), (none, tail))]
    slot = jnp.stack(slot_groups).reshape(len(slot_groups), devices * 8)

    early = [front, back] + x_one + y_one
    early_own, early_other = partials(own, other, early)
    early_got = moved(early_other, "ex", on_core)

    x_lent = moved(jnp.concatenate([v[:lent] for v in x_one], axis=0), "ex", on_z)
    y_lent = moved(jnp.concatenate([v[:lent] for v in y_one], axis=0), "ex", on_z)
    y_all = y_one[0] if side == 2 else jnp.concatenate(y_one, axis=0)
    x_all = x_one[0] if side == 2 else jnp.concatenate(x_one, axis=0)
    x_two = [moved(y_all, "pb", along_x(d)) for d in steps]
    y_two = [moved(x_all, "pb", along_y(d)) for d in steps]
    late_pieces = x_two + y_two + [x_lent, y_lent] + x_rest + y_rest
    late_own, late_other = partials(own, other, late_pieces)
    late_got = moved(late_other, "ex", on_core)

    my_x, my_y = me_pb % side, me_pb // side
    at = lambda dx, dy: ((my_y - dy) % side * side + (my_x - dx) % side) * block
    span = lambda start, count: start + jnp.arange(count, dtype=jnp.int32)
    columns = [span(at(0, 0) + first, half), span(at(0, 0) + second, half)]
    columns += [span(at(d, 0) + first, half) for d in steps]
    columns += [span(at(0, d) + second, half) for d in steps]
    for d in steps:
        columns += [span(at(d, up) + second, half) for up in steps]
    for up in steps:
        columns += [span(at(d, up) + first, half) for d in steps]
    columns += [span(at(d, 0) + second, lent) for d in steps]
    columns += [span(at(0, d) + first, lent) for d in steps]
    columns += [span(at(d, 0) + second + lent, half - lent) for d in steps]
    columns += [span(at(0, d) + first + lent, half - lent) for d in steps]
    column = jnp.concatenate(columns)[:, None]

    width = block * pb
    payload = full // 8 * width + (width // 2 if rest else 0)
    packed = pl.pallas_call(
        functools.partial(packed_kernel, full),
        out_shape=jax.ShapeDtypeStruct((devices * 8, payload), jnp.bfloat16),
        compiler_params=pltpu.CompilerParams(vmem_limit_bytes=48 << 20),
    )(early_own, early_got, late_own, late_got, residual[:, None], column, target)
    got = lax.all_to_all(packed.reshape(devices, 8, payload), BOTH, split_axis=0, concat_axis=0)
    return pl.pallas_call(
        functools.partial(table_kernel, full),
        out_shape=jax.ShapeDtypeStruct((table_rows, width), jnp.float32),
        compiler_params=pltpu.CompilerParams(vmem_limit_bytes=48 << 20),
    )(got.reshape(devices * 8, payload), slot)


def solution(mesh):
    return jax.shard_map(
        on_device,
        mesh=mesh,
        in_specs=(P(BOTH, None), P("pb", None), P(BOTH), P(BOTH), P()),
        out_specs=P(BOTH, None),
        check_vma=False,
    )
```

```python
import functools

import jax
import jax.numpy as jnp
from jax import lax
from jax.experimental import pallas as pl
from jax.experimental.pallas import tpu as pltpu
from jax.sharding import PartitionSpec as P

BOTH = ("ex", "pb")
NT = (((1,), (1,)), ((), ()))
TN = (((0,), (0,)), ((), ()))
LIMIT = pltpu.CompilerParams(vmem_limit_bytes=20 << 20)
FULL = pltpu.CompilerParams(vmem_limit_bytes=60 << 20)
LIGHT = pl.CostEstimate(flops=1, bytes_accessed=1, transcendentals=0)
HBM = pl.BlockSpec(memory_space=pltpu.HBM)
VMEM = pl.BlockSpec(memory_space=pltpu.VMEM)


def moved(value, axis, target):
    count = lax.axis_size(axis)
    return lax.ppermute(value, axis, [(i, target(i)) for i in range(count)])


def one_hot(hits):
    return jnp.where(hits, 1.0, 0.0).astype(jnp.bfloat16)


def pick(select, values):
    return jnp.dot(select, values, preferred_element_type=jnp.float32)


def scores_kernel(groups, count, *refs):
    held, sides = sum(groups), len(groups)
    rows, pieces, outs = refs[:held], refs[held : held + count], refs[held + count :]
    stack = lambda arrays: arrays[0][...] if len(arrays) == 1 else jnp.concatenate([a[...] for a in arrays], axis=0)
    total = lax.dot_general(stack(rows), stack(pieces), NT, preferred_element_type=jnp.float32)
    at = 0
    for out in outs:
        out[...] = total[at : at + out.shape[0]]
        at += out.shape[0]


def scored(groups, pieces):
    width = sum(piece.shape[0] for piece in pieces)
    arrays = [rows for group in groups for rows in group]
    shapes = [jax.ShapeDtypeStruct((sum(rows.shape[0] for rows in group), width), jnp.float32) for group in groups]
    return pl.pallas_call(
        functools.partial(scores_kernel, [len(group) for group in groups], len(pieces)),
        out_shape=shapes,
        compiler_params=LIMIT,
        cost_estimate=LIGHT,
    )(*arrays, *pieces)


def relayed(body, inputs, shapes, rooms, sems, limit):
    return pl.pallas_call(
        body,
        in_specs=[HBM] * len(inputs),
        out_specs=[HBM] * len(shapes),
        out_shape=[jax.ShapeDtypeStruct(shape, inputs[0].dtype) for shape in shapes],
        scratch_shapes=[pltpu.VMEM(room, inputs[0].dtype) for room in rooms] + [pltpu.SemaphoreType.DMA((sems,))],
        compiler_params=limit,
        cost_estimate=LIGHT,
    )(*inputs)


def relay(sems, plan):
    arriving, leaving, at = [], [], 0
    for source, room, _ in plan:
        arriving.append(pltpu.make_async_copy(source, room, sems.at[at]))
        arriving[-1].start()
        at += 1
    for copy, (_, room, targets) in zip(arriving, plan):
        copy.wait()
        for target in targets:
            leaving.append(pltpu.make_async_copy(room, target, sems.at[at]))
            leaving[-1].start()
            at += 1
    for copy in leaving:
        copy.wait()


def cut_queries(query, lent):
    half, deep = query.shape[0] // 2, query.shape[1] // 2
    ends = half - lent

    def body(query_ref, front_ref, back_ref, x_ref, y_ref, held, sems):
        core, layer = lax.axis_index("ex") % 2, lax.axis_index("ex") // 2 % 2
        columns = pl.ds(pl.multiple_of(core * deep, 128), deep)
        starts = [layer * half, half - layer * half]
        rows = lambda start, count: query_ref.at[pl.ds(pl.multiple_of(start, 16), count), columns]
        plan = []
        for side, (start, head) in enumerate(zip(starts, (front_ref, back_ref))):
            plan.append((rows(start, lent), held.at[side, pl.ds(0, lent)], [head]))
        for side, start in enumerate(starts):
            targets = [x_ref.at[pl.ds(side * ends, ends)], y_ref.at[pl.ds((1 - side) * ends, ends)]]
            plan.append((rows(start + lent, ends), held.at[side, pl.ds(lent, ends)], targets))
        relay(sems, plan)

    shapes = [(lent, deep)] * 2 + [(2 * ends, deep)] * 2
    return relayed(body, [query], shapes, [(2, half, deep)], 10, FULL)


def cut_examples(train, count):
    rows, deep = train.shape[0], train.shape[1] // 2
    height = rows // count

    def body(train_ref, own_ref, *others):
        core = lax.axis_index("ex") % 2
        for side in range(2):

            @pl.when(core == side)
            def _():
                own_ref[...] = train_ref[:, side * deep : (side + 1) * deep]
                for index, other in enumerate(others):
                    span = slice(index * height, (index + 1) * height)
                    other[...] = train_ref[span, (1 - side) * deep : (2 - side) * deep]

    shapes = [jax.ShapeDtypeStruct(shape, train.dtype) for shape in [(rows, deep)] + [(height, deep)] * count]
    own, *others = pl.pallas_call(body, out_shape=shapes, compiler_params=LIMIT, cost_estimate=LIGHT)(train)
    return own, others


def stacked(*outputs):
    arrays = []
    for output in outputs:
        for array, _, _ in output:
            if not any(array is known for known in arrays):
                arrays.append(array)
    index_of = lambda array: next(index for index, known in enumerate(arrays) if known is array)
    plans = [[(index_of(array), first, count) for array, first, count in output] for output in outputs]

    def body(*refs):
        for plan, out in zip(plans, refs[len(arrays) :]):
            at = 0
            for index, first, count in plan:
                out[at : at + count] = refs[index][first : first + count]
                at += count

    deep = arrays[0].shape[1]
    shapes = [jax.ShapeDtypeStruct((sum(p[2] for p in plan), deep), arrays[0].dtype) for plan in plans]
    return pl.pallas_call(body, out_shape=shapes, compiler_params=LIMIT, cost_estimate=LIGHT)(*arrays)


class Slots:
    def __init__(self, capacity, width, ids):
        self.width = width
        self.full, rest = capacity // 8, capacity % 8
        if rest > 4:
            self.full, rest = self.full + 1, 0
        self.half = width // 2 if rest else 0
        self.groups = self.full + (1 if rest else 0)
        self.at = self.full * width
        self.ids = self.at + self.half
        self.lanes = self.ids + (2 * self.groups if ids else 0)


def ordered(slots, scores, spans):
    rows, total, at = scores.shape[0], None, 0
    for base, count in spans:
        if base is not None:
            column = lax.broadcasted_iota(jnp.int32, (count, slots.width), 0) + base
            place = lax.broadcasted_iota(jnp.int32, (count, slots.width), 1)
            part = pick(scores[:, at : at + count], one_hot(place == column))
            total = part if total is None else total + part
        at += count
    return total


def weighted(own, got, scale):
    return ((own[...] if got is None else own[...] + got[...]) * scale[...]).astype(jnp.bfloat16)


def selects(slots, table_rows, height, placed_row, placed_column):
    rows = placed_row.shape[1]
    goal = placed_row[...] // table_rows
    same = placed_column[...] // table_rows == goal
    before = lax.broadcasted_iota(jnp.int32, (rows, rows), 0) < lax.broadcasted_iota(jnp.int32, (rows, rows), 1)
    rank = jnp.sum(jnp.where(same & before, 1, 0), axis=0, keepdims=True)
    row = lax.broadcasted_iota(jnp.int32, (height, rows), 0)
    found = [one_hot(row == jnp.where(rank // 8 == index, goal * 8 + rank % 8, -1)) for index in range(slots.full)]
    if slots.half:
        late = rank - slots.full * 8
        found += [one_hot(row == jnp.where(late >= 0, goal * 8 + side * 4 + late, -1)) for side in range(2)]
    return found


def digits(slots, table_rows, placed_column):
    number = placed_column[...] % table_rows + 1
    lane = lax.broadcasted_iota(jnp.int32, (number.shape[0], 2 * slots.groups), 1)
    digit = jnp.where(lane % 2 == 0, number // 128, number % 128)
    kept = [jnp.where(lane // 2 == index, digit, 0) for index in range(slots.groups)]
    return [value.astype(jnp.float32).astype(jnp.bfloat16) for value in kept]


def put(slots, found, table, out_ref, ids=None, base_ref=None):
    table = table.astype(jnp.bfloat16)

    def write(start, values):
        values, span = values.astype(jnp.bfloat16), slice(start, start + values.shape[1])
        out_ref[:, span] = values if base_ref is None else values + base_ref[:, span]

    for index in range(slots.full):
        write(index * slots.width, pick(found[index], table))
    if slots.half:
        left, right = (pick(found[slots.full + i], table[:, i * slots.half : (i + 1) * slots.half]) for i in range(2))
        write(slots.at, left + right)
    if ids is not None:
        pairs = [(found[index], ids[min(index, slots.full)]) for index in range(len(found))]
        write(slots.ids, sum(pick(select, digit) for select, digit in pairs))


def called(body, shapes, *operands):
    return pl.pallas_call(body, out_shape=shapes, compiler_params=LIMIT, cost_estimate=LIGHT)(*operands)


def exchanged(rows, devices):
    apart = rows.reshape(devices, 8, rows.shape[1])
    return lax.all_to_all(apart, BOTH, split_axis=0, concat_axis=0).reshape(rows.shape)


def received(slots, ref, index):
    if index < slots.full:
        return ref[:, index * slots.width : (index + 1) * slots.width]
    half = ref[:, slots.at : slots.at + slots.half]
    row = lax.broadcasted_iota(jnp.int32, (half.shape[0], slots.width), 0)
    lane = lax.broadcasted_iota(jnp.int32, (half.shape[0], slots.width), 1)
    return jnp.where((row % 8 < 4) == (lane < slots.half), jnp.concatenate([half, half], axis=1), 0)


def places(pb, count, width):
    sender = lax.broadcasted_iota(jnp.int32, (count, width), 0) // 8 % pb
    return sender, lax.broadcasted_iota(jnp.int32, (count, width), 1) // (width // pb)


def first_table_kernel(slots, pb, table_rows, got_ref, out_ref, hot_ref=None):
    count, width = got_ref.shape[0], out_ref.shape[1]
    entry = lax.broadcasted_iota(jnp.int32, (count, table_rows), 1)
    total = None
    for index in range(slots.groups):
        at = slots.ids + 2 * index
        number = got_ref[:, at : at + 2].astype(jnp.float32)
        hot = one_hot(entry == (number[:, 0:1] * 128.0 + number[:, 1:2]).astype(jnp.int32) - 1)
        values = received(slots, got_ref, index)
        if hot_ref is not None:
            hot_ref[index] = hot
            sender, lane = places(pb, count, width)
            values = jnp.where(sender == lane, jnp.concatenate([values] * pb, axis=1), 0)
        part = lax.dot_general(hot, values, TN, preferred_element_type=jnp.float32)
        total = part if total is None else total + part
    out_ref[...] = total


def last_table_kernel(slots, pb, first_ref, hot_ref, got_ref, out_ref):
    count, width = got_ref.shape[0], out_ref.shape[1]
    total = first_ref[...]
    sender, lane = places(pb, count, width)
    for index in range(slots.groups):
        values = received(slots, got_ref, index)
        none = jnp.zeros((count, width - slots.width), values.dtype)
        below, above = jnp.concatenate([values, none], axis=1), jnp.concatenate([none, values], axis=1)
        values = jnp.where(lane < sender, below, jnp.where(lane > sender, above, 0))
        total += lax.dot_general(hot_ref[index], values, TN, preferred_element_type=jnp.float32)
    out_ref[...] = total


def on_device(train, query, residual, example_source, source_place):
    rows, depth = train.shape
    block = query.shape[0]
    ex, pb = lax.axis_size("ex"), lax.axis_size("pb")
    me_ex, me_pb = lax.axis_index("ex"), lax.axis_index("pb")
    devices = ex * pb
    table_rows = source_place.shape[0] // devices
    capacity = max(1, -(-2 * rows // devices))
    core, layer = me_ex % 2, (me_ex // 2) % 2
    deep = depth // 2
    on_core = lambda i: i ^ 1
    on_z = lambda i: i ^ 2
    on_x = lambda i: i ^ 1
    on_y = lambda i: i ^ 2
    scale = residual[:, None]
    whole = jax.ShapeDtypeStruct((table_rows, block * pb), jnp.float32)

    placed = jnp.take(source_place, example_source)
    places = placed[None, :], placed[:, None]
    packed_rows = lambda slots: jax.ShapeDtypeStruct((devices * 8, slots.lanes), jnp.bfloat16)

    if pb != 4 or ex % 4 != 0:
        other = moved(lax.dynamic_slice(train, (0, (1 - core) * deep), (rows, deep)), "ex", on_core)
        own = lax.dynamic_slice(train, (0, core * deep), (rows, deep))
        queries = lax.all_gather(lax.dynamic_slice(query, (0, core * deep), (block, deep)), "pb", tiled=True)
        slots = Slots(capacity, block * pb, True)
        own, other = scored([[own], [other]], [queries])

        def pack(own_ref, got_ref, scale_ref, row_ref, column_ref, out_ref):
            found = selects(slots, table_rows, devices * 8, row_ref, column_ref)
            put(slots, found, weighted(own_ref, got_ref, scale_ref), out_ref, digits(slots, table_rows, column_ref))

        got = exchanged(called(pack, packed_rows(slots), own, moved(other, "ex", on_core), scale, *places), devices)
        return called(functools.partial(first_table_kernel, slots, pb, table_rows), whole, got)

    half = block // 2
    lent = half * 2 // 3 // 16 * 16
    ends = half - lent
    front, back, x_sent, y_sent = cut_queries(query, lent)
    x_one = moved(front, "pb", on_x)
    y_one = moved(back, "pb", on_y)
    x_end = moved(x_sent, "pb", on_x)
    y_end = moved(y_sent, "pb", on_y)
    early, late = Slots(capacity, block, True), Slots(capacity, block * (pb - 1), False)

    def own_pack(scores_ref, scale_ref, row_ref, column_ref, out_ref):
        found = selects(early, table_rows, devices * 8, row_ref, column_ref)
        put(early, found, weighted(scores_ref, None, scale_ref), out_ref, digits(early, table_rows, column_ref))

    def spans(wanted):
        me, layer = lax.axis_index("pb"), lax.axis_index("ex") // 2 % 2
        x, y = me % 2, me // 2
        blocks = {"x": y * 2 + 1 - x, "y": (1 - y) * 2 + x, "xy": (1 - y) * 2 + 1 - x}
        starts = {"first": layer * half, "second": half - layer * half}
        place = lambda other: (other - jnp.where(other > me, 1, 0)) * block
        return [(place(blocks[over]) + starts[part] + start, count) for over, part, start, count in wanted]

    def near_pack(own_ref, got_ref, scale_ref, row_ref, column_ref, out_ref):
        found = selects(late, table_rows, devices * 8, row_ref, column_ref)
        put(late, found, ordered(late, weighted(own_ref, got_ref, scale_ref), spans(near)), out_ref)

    def far_pack(own_ref, got_ref, scale_ref, row_ref, column_ref, base_ref, out_ref):
        found = selects(late, table_rows, devices * 8, row_ref, column_ref)
        put(late, found, ordered(late, weighted(own_ref, got_ref, scale_ref), spans(far)), out_ref, None, base_ref)

    (scores_own,) = scored([[train]], [query])
    rows_own = called(own_pack, packed_rows(early), scores_own, scale, *places)
    train, rows_own = lax.optimization_barrier((train, rows_own))
    sent_own = exchanged(rows_own, devices)
    own, others = cut_examples(train, 4)
    others = [moved(part, "ex", on_core) for part in others]

    ahead = lent * 3 // 4 // 16 * 16
    z_sent, x_sent, y_sent = stacked([(x_one, 0, lent), (y_one, 0, lent)], [(y_one, 0, ahead)], [(x_one, 0, ahead)])
    z_lent = moved(z_sent, "ex", on_z)
    x_two = moved(x_sent, "pb", on_x)
    y_two = moved(y_sent, "pb", on_y)
    x_sent, y_sent = stacked(
        [(y_one, ahead, lent - ahead), (y_end, 0, ends)], [(x_one, ahead, lent - ahead), (x_end, 0, ends)]
    )
    x_last = moved(x_sent, "pb", on_x)
    y_last = moved(y_sent, "pb", on_y)

    near = [
        ("x", "first", 0, lent),
        ("y", "second", 0, lent),
        ("x", "first", lent, ends),
        ("x", "second", lent, ends),
        ("y", "second", lent, ends),
        ("y", "first", lent, ends),
        ("xy", "second", 0, ahead),
        ("xy", "first", 0, ahead),
    ]
    far = [
        ("xy", "second", ahead, lent - ahead),
        ("xy", "second", lent, ends),
        ("xy", "first", ahead, lent - ahead),
        ("xy", "first", lent, ends),
        ("x", "second", 0, lent),
        ("y", "first", 0, lent),
    ]
    own_a, other_a = scored([[own], others], [x_one, y_one, x_end, y_end, x_two, y_two])
    got_a = moved(other_a, "ex", on_core)
    base = called(near_pack, packed_rows(late), own_a, got_a, scale, *places)
    own, others, base, sent_own = lax.optimization_barrier((own, others, base, sent_own))
    (other_b,) = scored([others], [x_last, y_last, z_lent])
    got_b = moved(other_b, "ex", on_core)
    (own_b,) = scored([[own]], [x_last, y_last, z_lent])
    sent = exchanged(called(far_pack, packed_rows(late), own_b, got_b, scale, *places, base), devices)

    hot = jax.ShapeDtypeStruct((early.groups, devices * 8, table_rows), jnp.bfloat16)
    table, hot = called(functools.partial(first_table_kernel, early, pb, table_rows), [whole, hot], sent_own)
    return called(functools.partial(last_table_kernel, late, pb), whole, table, hot, sent)


def solution(mesh):
    return jax.shard_map(
        on_device,
        mesh=mesh,
        in_specs=(P(BOTH, None), P("pb", None), P(BOTH), P(BOTH), P()),
        out_specs=P(BOTH, None),
        check_vma=False,
    )
```

```python
import functools

import jax
import jax.numpy as jnp
from jax import lax
from jax.experimental import pallas as pl
from jax.experimental.pallas import tpu as pltpu
from jax.sharding import PartitionSpec as P

BOTH = ("ex", "pb")
NT = (((1,), (1,)), ((), ()))
TN = (((0,), (0,)), ((), ()))
LIMIT = pltpu.CompilerParams(vmem_limit_bytes=20 << 20)
FULL = pltpu.CompilerParams(vmem_limit_bytes=60 << 20)
LIGHT = pl.CostEstimate(flops=1, bytes_accessed=1, transcendentals=0)
HBM = pl.BlockSpec(memory_space=pltpu.HBM)
VMEM = pl.BlockSpec(memory_space=pltpu.VMEM)


def moved(value, axis, target):
    count = lax.axis_size(axis)
    return lax.ppermute(value, axis, [(i, target(i)) for i in range(count)])


def one_hot(hits):
    return jnp.where(hits, 1.0, 0.0).astype(jnp.bfloat16)


def pick(select, values):
    return jnp.dot(select, values, preferred_element_type=jnp.float32)


def scores_kernel(groups, count, *refs):
    held, sides = sum(groups), len(groups)
    rows, pieces, outs = refs[:held], refs[held : held + count], refs[held + count :]
    stack = lambda arrays: arrays[0][...] if len(arrays) == 1 else jnp.concatenate([a[...] for a in arrays], axis=0)
    total = lax.dot_general(stack(rows), stack(pieces), NT, preferred_element_type=jnp.float32)
    at = 0
    for out in outs:
        out[...] = total[at : at + out.shape[0]]
        at += out.shape[0]


def scored(groups, pieces):
    width = sum(piece.shape[0] for piece in pieces)
    arrays = [rows for group in groups for rows in group]
    shapes = [jax.ShapeDtypeStruct((sum(rows.shape[0] for rows in group), width), jnp.float32) for group in groups]
    return pl.pallas_call(
        functools.partial(scores_kernel, [len(group) for group in groups], len(pieces)),
        out_shape=shapes,
        compiler_params=LIMIT,
        cost_estimate=LIGHT,
    )(*arrays, *pieces)


def relayed(body, inputs, shapes, rooms, sems, limit):
    return pl.pallas_call(
        body,
        in_specs=[HBM] * len(inputs),
        out_specs=[HBM] * len(shapes),
        out_shape=[jax.ShapeDtypeStruct(shape, inputs[0].dtype) for shape in shapes],
        scratch_shapes=[pltpu.VMEM(room, inputs[0].dtype) for room in rooms] + [pltpu.SemaphoreType.DMA((sems,))],
        compiler_params=limit,
        cost_estimate=LIGHT,
    )(*inputs)


def relay(sems, plan):
    arriving, leaving, at = [], [], 0
    for source, room, _ in plan:
        arriving.append(pltpu.make_async_copy(source, room, sems.at[at]))
        arriving[-1].start()
        at += 1
    for copy, (_, room, targets) in zip(arriving, plan):
        copy.wait()
        for target in targets:
            leaving.append(pltpu.make_async_copy(room, target, sems.at[at]))
            leaving[-1].start()
            at += 1
    for copy in leaving:
        copy.wait()


def cut_inputs(query, train, lent, count):
    half, deep, rows = query.shape[0] // 2, query.shape[1] // 2, train.shape[0]
    ends = half - lent

    def body(query_ref, train_ref, front_ref, back_ref, front_end_ref, back_end_ref, *refs):
        other_refs, (held, kept, sems) = refs[:count], refs[count:]
        core, layer = lax.axis_index("ex") % 2, lax.axis_index("ex") // 2 % 2
        mine = pl.ds(pl.multiple_of(core * deep, 128), deep)
        theirs = pl.ds(pl.multiple_of(deep - core * deep, 128), deep)
        starts = [layer * half, half - layer * half]
        part = lambda start, count: query_ref.at[pl.ds(pl.multiple_of(start, 16), count), mine]
        wholes, tails = (front_ref, back_ref), (front_end_ref, back_end_ref)
        plan = []
        for side in range(2):
            for first, height in ((0, lent), (lent, ends)):
                span = pl.ds(first, height)
                targets = [wholes[side].at[span]] + ([tails[side]] if first else [])
                plan.append((part(starts[side] + first, height), held.at[side, span], targets))
        for index, other_ref in enumerate(other_refs):
            span = pl.ds(index * (rows // count), rows // count)
            plan.append((train_ref.at[span, theirs], kept.at[span], [other_ref]))
        relay(sems, plan)

    shapes = [(half, deep)] * 2 + [(ends, deep)] * 2 + [(rows // count, deep)] * count
    return relayed(body, [query, train], shapes, [(2, half, deep), (rows, deep)], 10 + 2 * count, FULL)


def stacked(*outputs):
    arrays = []
    for output in outputs:
        for array, _, _ in output:
            if not any(array is known for known in arrays):
                arrays.append(array)
    index_of = lambda array: next(index for index, known in enumerate(arrays) if known is array)
    plans = [[(index_of(array), first, count) for array, first, count in output] for output in outputs]

    def body(*refs):
        for plan, out in zip(plans, refs[len(arrays) :]):
            at = 0
            for index, first, count in plan:
                out[at : at + count] = refs[index][first : first + count]
                at += count

    deep = arrays[0].shape[1]
    shapes = [jax.ShapeDtypeStruct((sum(p[2] for p in plan), deep), arrays[0].dtype) for plan in plans]
    return pl.pallas_call(body, out_shape=shapes, compiler_params=LIMIT, cost_estimate=LIGHT)(*arrays)


class Slots:
    def __init__(self, capacity, width, ids):
        self.width = width
        self.full, rest = capacity // 8, capacity % 8
        if rest > 4:
            self.full, rest = self.full + 1, 0
        self.half = width // 2 if rest else 0
        self.groups = self.full + (1 if rest else 0)
        self.at = self.full * width
        self.ids = self.at + self.half
        self.lanes = self.ids + (2 * self.groups if ids else 0)


def ordered(slots, scores, spans):
    rows, total, at = scores.shape[0], None, 0
    for base, count in spans:
        if base is not None:
            column = lax.broadcasted_iota(jnp.int32, (count, slots.width), 0) + base
            place = lax.broadcasted_iota(jnp.int32, (count, slots.width), 1)
            part = pick(scores[:, at : at + count], one_hot(place == column))
            total = part if total is None else total + part
        at += count
    return total


def upright(row):
    count = row.shape[1]
    diagonal = lax.broadcasted_iota(jnp.int32, (count, count), 0) == lax.broadcasted_iota(jnp.int32, (count, count), 1)
    return jnp.sum(jnp.where(diagonal, row, jnp.zeros_like(row)), axis=1, keepdims=True)


def packing(body, shape, residual, placed, *operands):
    rows = residual.shape[0]

    def kernel(scale_ref, row_ref, *refs):
        *refs, scale, row, sems = refs
        copies = [pltpu.make_async_copy(scale_ref, scale, sems.at[0]), pltpu.make_async_copy(row_ref, row, sems.at[1])]
        for copy in copies:
            copy.start()
        for copy in copies:
            copy.wait()
        body(scale[...], row[...], *refs)

    return pl.pallas_call(
        kernel,
        in_specs=[HBM] * 2 + [VMEM] * len(operands),
        out_shape=shape,
        scratch_shapes=[
            pltpu.VMEM((1, rows), residual.dtype),
            pltpu.VMEM((1, rows), placed.dtype),
            pltpu.SemaphoreType.DMA((2,)),
        ],
        compiler_params=LIMIT,
        cost_estimate=LIGHT,
    )(residual[None, :], placed[None, :], *operands)


def weighted(own, got, scale):
    return ((own[...] if got is None else own[...] + got[...]) * upright(scale)).astype(jnp.bfloat16)


def selects(slots, table_rows, height, placed):
    rows = placed.shape[1]
    goal = placed // table_rows
    same = upright(goal) == goal
    before = lax.broadcasted_iota(jnp.int32, (rows, rows), 0) < lax.broadcasted_iota(jnp.int32, (rows, rows), 1)
    rank = jnp.sum(jnp.where(same & before, 1, 0), axis=0, keepdims=True)
    row = lax.broadcasted_iota(jnp.int32, (height, rows), 0)
    found = [one_hot(row == jnp.where(rank // 8 == index, goal * 8 + rank % 8, -1)) for index in range(slots.full)]
    if slots.half:
        late = rank - slots.full * 8
        found += [one_hot(row == jnp.where(late >= 0, goal * 8 + side * 4 + late, -1)) for side in range(2)]
    return found


def digits(slots, table_rows, placed):
    number = upright(placed % table_rows + 1)
    lane = lax.broadcasted_iota(jnp.int32, (number.shape[0], 2 * slots.groups), 1)
    digit = jnp.where(lane % 2 == 0, number // 128, number % 128)
    kept = [jnp.where(lane // 2 == index, digit, 0) for index in range(slots.groups)]
    return [value.astype(jnp.float32).astype(jnp.bfloat16) for value in kept]


def put(slots, found, table, out_ref, ids=None, base_ref=None):
    table = table.astype(jnp.bfloat16)

    def write(start, values):
        values, span = values.astype(jnp.bfloat16), slice(start, start + values.shape[1])
        out_ref[:, span] = values if base_ref is None else values + base_ref[:, span]

    for index in range(slots.full):
        write(index * slots.width, pick(found[index], table))
    if slots.half:
        left, right = (pick(found[slots.full + i], table[:, i * slots.half : (i + 1) * slots.half]) for i in range(2))
        write(slots.at, left + right)
    if ids is not None:
        pairs = [(found[index], ids[min(index, slots.full)]) for index in range(len(found))]
        write(slots.ids, sum(pick(select, digit) for select, digit in pairs))


def called(body, shapes, *operands):
    return pl.pallas_call(body, out_shape=shapes, compiler_params=LIMIT, cost_estimate=LIGHT)(*operands)


def exchanged(rows, devices):
    apart = rows.reshape(devices, 8, rows.shape[1])
    return lax.all_to_all(apart, BOTH, split_axis=0, concat_axis=0).reshape(rows.shape)


def halves(slots, pb, count):
    row = lax.broadcasted_iota(jnp.int32, (count, slots.width), 0)
    unit = lax.broadcasted_iota(jnp.int32, (count, slots.width), 1) // (slots.width // 4)
    peer = row // 8
    y, x, layer = peer // 2 % 2, peer % 2, peer // pb // 2 % 2
    apart = (unit // 2 != (x + y) % 2) & (unit % 2 != layer)
    return (y == 0) != apart


def added(slots, totals, hot, ref, index, lower):
    if index < slots.full:
        values = ref[:, index * slots.width : (index + 1) * slots.width]
    else:
        half = ref[:, slots.at : slots.at + slots.half]
        row = lax.broadcasted_iota(jnp.int32, (half.shape[0], slots.width), 0)
        lane = lax.broadcasted_iota(jnp.int32, (half.shape[0], slots.width), 1)
        values = jnp.where((row % 8 < 4) == (lane < slots.half), jnp.concatenate([half, half], axis=1), 0)
    values = [values] if lower is None else [jnp.where(lower, values, 0), jnp.where(lower, 0, values)]
    parts = [lax.dot_general(hot, v, TN, preferred_element_type=jnp.float32) for v in values]
    return parts if totals is None else [t + p for t, p in zip(totals, parts)]


def first_table_kernel(slots, pb, table_rows, split, got_ref, out_ref, hot_ref=None):
    count = got_ref.shape[0]
    lower = halves(slots, pb, count) if split else None
    entry = lax.broadcasted_iota(jnp.int32, (count, table_rows), 1)
    totals = None
    for index in range(slots.groups):
        at = slots.ids + 2 * index
        number = got_ref[:, at : at + 2].astype(jnp.float32)
        hot = one_hot(entry == (number[:, 0:1] * 128.0 + number[:, 1:2]).astype(jnp.int32) - 1)
        if hot_ref is not None:
            hot_ref[index] = hot
        totals = added(slots, totals, hot, got_ref, index, lower)
    for side, total in enumerate(totals):
        out_ref[:, side * slots.width : (side + 1) * slots.width] = total


def last_table_kernel(slots, pb, first_ref, hot_ref, got_ref, out_ref):
    width, half = slots.width, slots.width // 2
    upper = jnp.logical_not(halves(slots, pb, got_ref.shape[0]))
    totals = None
    for index in range(slots.groups):
        totals = added(slots, totals, hot_ref[index], got_ref, index, upper)
    out_ref[:, :width] = first_ref[:, :width] + totals[0]
    above = first_ref[:, width:] + totals[1]
    out_ref[:, width : width + half] = above[:, half:]
    out_ref[:, width + half :] = above[:, :half]


def on_device(train, query, residual, example_source, source_place):
    rows, depth = train.shape
    block = query.shape[0]
    ex, pb = lax.axis_size("ex"), lax.axis_size("pb")
    me_ex, me_pb = lax.axis_index("ex"), lax.axis_index("pb")
    devices = ex * pb
    table_rows = source_place.shape[0] // devices
    capacity = max(1, -(-2 * rows // devices))
    core, layer = me_ex % 2, (me_ex // 2) % 2
    deep = depth // 2
    on_core = lambda i: i ^ 1
    on_z = lambda i: i ^ 2
    on_x = lambda i: i ^ 1
    on_y = lambda i: i ^ 2
    whole = jax.ShapeDtypeStruct((table_rows, block * pb), jnp.float32)

    placed = jnp.take(source_place, example_source)
    packed_rows = lambda slots: jax.ShapeDtypeStruct((devices * 8, slots.lanes), jnp.bfloat16)

    if pb != 4 or ex % 4 != 0:
        other = moved(lax.dynamic_slice(train, (0, (1 - core) * deep), (rows, deep)), "ex", on_core)
        own = lax.dynamic_slice(train, (0, core * deep), (rows, deep))
        queries = lax.all_gather(lax.dynamic_slice(query, (0, core * deep), (block, deep)), "pb", tiled=True)
        slots = Slots(capacity, block * pb, True)
        own, other = scored([[own], [other]], [queries])

        def pack(scale, row, own_ref, got_ref, out_ref):
            found = selects(slots, table_rows, devices * 8, row)
            put(slots, found, weighted(own_ref, got_ref, scale), out_ref, digits(slots, table_rows, row))

        got = exchanged(packing(pack, packed_rows(slots), residual, placed, own, moved(other, "ex", on_core)), devices)
        return called(functools.partial(first_table_kernel, slots, pb, table_rows, False), whole, got)

    half = block // 2
    lent = half // 2 // 16 * 16
    ends = half - lent
    front, back, front_end, back_end, *others = cut_inputs(query, train, lent, 4)
    x_one = moved(front, "pb", on_x)
    y_one = moved(back, "pb", on_y)
    x_end = moved(back_end, "pb", on_x)
    y_end = moved(front_end, "pb", on_y)

    early, late = Slots(capacity, 2 * block, True), Slots(capacity, 2 * block, False)

    def units():
        me, layer = lax.axis_index("pb"), lax.axis_index("ex") // 2 % 2
        same = (me % 2 + me // 2) % 2
        unit = lambda near, part: (2 * (same if near else 1 - same) + part) * half
        return unit, layer, 1 - layer

    def first_pack(scale, row, home_ref, own_ref, got_ref, out_ref, base_ref):
        unit, mine, theirs = units()
        found = selects(early, table_rows, devices * 8, row)
        near = weighted(own_ref, got_ref, scale)
        table = ordered(early, weighted(home_ref, None, scale), [(unit(True, 0), block)])
        table += ordered(early, near, [(unit(False, mine), half), (unit(False, theirs), half)])
        put(early, found, table, out_ref, digits(early, table_rows, row))
        left = [(None, 2 * half), (unit(False, theirs) + lent, ends), (unit(False, mine) + lent, ends)]
        put(late, found, ordered(late, near, left), base_ref)

    def last_pack(scale, row, own_ref, got_ref, base_ref, out_ref):
        unit, mine, theirs = units()
        found = selects(late, table_rows, devices * 8, row)
        spans = [(unit(True, theirs), half), (unit(True, mine), half)]
        spans += [(unit(False, theirs), lent), (unit(False, mine), lent)]
        put(late, found, ordered(late, weighted(own_ref, got_ref, scale), spans), out_ref, None, base_ref)

    others = [moved(part, "ex", on_core) for part in others]
    own = lax.dynamic_slice(train, (0, core * deep), (rows, deep))
    (scores_own,) = scored([[train]], [query])
    x_one, y_one, others, own, scores_own, placed = lax.optimization_barrier(
        (x_one, y_one, others, own, scores_own, placed)
    )

    (z_sent,) = stacked([(x_one, 0, lent), (y_one, 0, lent)])
    z_lent = moved(z_sent, "ex", on_z)
    x_two = moved(y_one, "pb", on_x)
    y_two = moved(x_one, "pb", on_y)

    own_a, other_a = scored([[own], others], [x_one, y_one, x_end, y_end])
    got_a = moved(other_a, "ex", on_core)
    shapes = [packed_rows(early), packed_rows(late)]
    rows_a, base = packing(first_pack, shapes, residual, placed, scores_own, own_a, got_a)
    sent_a = exchanged(rows_a, devices)
    own, others, base = lax.optimization_barrier((own, others, base))

    pieces = [x_two, y_two, z_lent]
    (other_b,) = scored([others], pieces)
    got_b = moved(other_b, "ex", on_core)
    (own_b,) = scored([[own]], pieces)
    sent_b = exchanged(packing(last_pack, packed_rows(late), residual, placed, own_b, got_b, base), devices)

    hot = jax.ShapeDtypeStruct((early.groups, devices * 8, table_rows), jnp.bfloat16)
    table, hot = called(functools.partial(first_table_kernel, early, pb, table_rows, True), [whole, hot], sent_a)
    return called(functools.partial(last_table_kernel, late, pb), whole, table, hot, sent_b)


def solution(mesh):
    return jax.shard_map(
        on_device,
        mesh=mesh,
        in_specs=(P(BOTH, None), P("pb", None), P(BOTH), P(BOTH), P()),
        out_specs=P(BOTH, None),
        check_vma=False,
    )
```

```python
import functools

import jax
import jax.numpy as jnp
from jax import lax
from jax.experimental import pallas as pl
from jax.experimental.pallas import tpu as pltpu
from jax.sharding import PartitionSpec as P

BOTH = ("ex", "pb")
NT = (((1,), (1,)), ((), ()))
TN = (((0,), (0,)), ((), ()))
LIMIT = pltpu.CompilerParams(vmem_limit_bytes=20 << 20)
FULL = pltpu.CompilerParams(vmem_limit_bytes=60 << 20)
LIGHT = pl.CostEstimate(flops=1, bytes_accessed=1, transcendentals=0)
HBM = pl.BlockSpec(memory_space=pltpu.HBM)
VMEM = pl.BlockSpec(memory_space=pltpu.VMEM)


def moved(value, axis, target):
    count = lax.axis_size(axis)
    return lax.ppermute(value, axis, [(i, target(i)) for i in range(count)])


def one_hot(hits):
    return jnp.where(hits, 1.0, 0.0).astype(jnp.bfloat16)


def pick(select, values):
    return jnp.dot(select, values, preferred_element_type=jnp.float32)


def scores_kernel(groups, count, *refs):
    held, sides = sum(groups), len(groups)
    rows, pieces, outs = refs[:held], refs[held : held + count], refs[held + count :]
    stack = lambda arrays: arrays[0][...] if len(arrays) == 1 else jnp.concatenate([a[...] for a in arrays], axis=0)
    total = lax.dot_general(stack(rows), stack(pieces), NT, preferred_element_type=jnp.float32)
    at = 0
    for out in outs:
        out[...] = total[at : at + out.shape[0]]
        at += out.shape[0]


def scored(groups, pieces):
    width = sum(piece.shape[0] for piece in pieces)
    arrays = [rows for group in groups for rows in group]
    shapes = [jax.ShapeDtypeStruct((sum(rows.shape[0] for rows in group), width), jnp.float32) for group in groups]
    return pl.pallas_call(
        functools.partial(scores_kernel, [len(group) for group in groups], len(pieces)),
        out_shape=shapes,
        compiler_params=LIMIT,
        cost_estimate=LIGHT,
    )(*arrays, *pieces)


def relayed(body, inputs, shapes, rooms, sems, limit):
    return pl.pallas_call(
        body,
        in_specs=[HBM] * len(inputs),
        out_specs=[HBM] * len(shapes),
        out_shape=[jax.ShapeDtypeStruct(shape, inputs[0].dtype) for shape in shapes],
        scratch_shapes=[pltpu.VMEM(room, inputs[0].dtype) for room in rooms] + [pltpu.SemaphoreType.DMA((sems,))],
        compiler_params=limit,
        cost_estimate=LIGHT,
    )(*inputs)


def relay(sems, plan):
    arriving, leaving, at = [], [], 0
    for source, room, _ in plan:
        arriving.append(pltpu.make_async_copy(source, room, sems.at[at]))
        arriving[-1].start()
        at += 1
    for copy, (_, room, targets) in zip(arriving, plan):
        copy.wait()
        for target in targets:
            leaving.append(pltpu.make_async_copy(room, target, sems.at[at]))
            leaving[-1].start()
            at += 1
    for copy in leaving:
        copy.wait()


def cut_inputs(query, train, lent, count):
    half, deep, rows = query.shape[0] // 2, query.shape[1] // 2, train.shape[0]
    ends = half - lent

    def body(query_ref, train_ref, front_ref, back_ref, front_end_ref, back_end_ref, *refs):
        other_refs, (held, kept, sems) = refs[:count], refs[count:]
        core, layer = lax.axis_index("ex") % 2, lax.axis_index("ex") // 2 % 2
        mine = pl.ds(pl.multiple_of(core * deep, 128), deep)
        theirs = pl.ds(pl.multiple_of(deep - core * deep, 128), deep)
        starts = [layer * half, half - layer * half]
        part = lambda start, count: query_ref.at[pl.ds(pl.multiple_of(start, 16), count), mine]
        wholes, tails = (front_ref, back_ref), (front_end_ref, back_end_ref)
        plan = []
        for side in range(2):
            for first, height in ((0, lent), (lent, ends)):
                span = pl.ds(first, height)
                targets = [wholes[side].at[span]] + ([tails[side]] if first else [])
                plan.append((part(starts[side] + first, height), held.at[side, span], targets))
        for index, other_ref in enumerate(other_refs):
            span = pl.ds(index * (rows // count), rows // count)
            plan.append((train_ref.at[span, theirs], kept.at[span], [other_ref]))
        relay(sems, plan)

    shapes = [(half, deep)] * 2 + [(ends, deep)] * 2 + [(rows // count, deep)] * count
    return relayed(body, [query, train], shapes, [(2, half, deep), (rows, deep)], 10 + 2 * count, FULL)


def stacked(*outputs):
    arrays = []
    for output in outputs:
        for array, _, _ in output:
            if not any(array is known for known in arrays):
                arrays.append(array)
    index_of = lambda array: next(index for index, known in enumerate(arrays) if known is array)
    plans = [[(index_of(array), first, count) for array, first, count in output] for output in outputs]

    def body(*refs):
        for plan, out in zip(plans, refs[len(arrays) :]):
            at = 0
            for index, first, count in plan:
                out[at : at + count] = refs[index][first : first + count]
                at += count

    deep = arrays[0].shape[1]
    shapes = [jax.ShapeDtypeStruct((sum(p[2] for p in plan), deep), arrays[0].dtype) for plan in plans]
    return pl.pallas_call(body, out_shape=shapes, compiler_params=LIMIT, cost_estimate=LIGHT)(*arrays)


class Slots:
    def __init__(self, capacity, width, ids):
        self.width = width
        self.full, rest = capacity // 8, capacity % 8
        if rest > 4:
            self.full, rest = self.full + 1, 0
        self.half = width // 2 if rest else 0
        self.groups = self.full + (1 if rest else 0)
        self.at = self.full * width
        self.ids = self.at + self.half
        self.lanes = self.ids + (2 * self.groups if ids else 0)


def ordered(slots, scores, spans):
    rows, total, at = scores.shape[0], None, 0
    for base, count in spans:
        if base is not None:
            column = lax.broadcasted_iota(jnp.int32, (count, slots.width), 0) + base
            place = lax.broadcasted_iota(jnp.int32, (count, slots.width), 1)
            part = pick(scores[:, at : at + count], one_hot(place == column))
            total = part if total is None else total + part
        at += count
    return total


def upright(row):
    count = row.shape[1]
    diagonal = lax.broadcasted_iota(jnp.int32, (count, count), 0) == lax.broadcasted_iota(jnp.int32, (count, count), 1)
    return jnp.sum(jnp.where(diagonal, row, jnp.zeros_like(row)), axis=1, keepdims=True)


def packing(body, shape, residual, placed, *operands):
    rows = residual.shape[0]

    def kernel(scale_ref, row_ref, *refs):
        *refs, scale, row, sems = refs
        copies = [pltpu.make_async_copy(scale_ref, scale, sems.at[0]), pltpu.make_async_copy(row_ref, row, sems.at[1])]
        for copy in copies:
            copy.start()
        for copy in copies:
            copy.wait()
        body(scale[...], row[...], *refs)

    return pl.pallas_call(
        kernel,
        in_specs=[HBM] * 2 + [VMEM] * len(operands),
        out_shape=shape,
        scratch_shapes=[
            pltpu.VMEM((1, rows), residual.dtype),
            pltpu.VMEM((1, rows), placed.dtype),
            pltpu.SemaphoreType.DMA((2,)),
        ],
        compiler_params=LIMIT,
        cost_estimate=LIGHT,
    )(residual[None, :], placed[None, :], *operands)


def weighted(own, got, scale):
    return ((own[...] if got is None else own[...] + got[...]) * upright(scale)).astype(jnp.bfloat16)


def selects(slots, table_rows, height, placed):
    rows = placed.shape[1]
    goal = placed // table_rows
    same = upright(goal) == goal
    before = lax.broadcasted_iota(jnp.int32, (rows, rows), 0) < lax.broadcasted_iota(jnp.int32, (rows, rows), 1)
    rank = jnp.sum(jnp.where(same & before, 1, 0), axis=0, keepdims=True)
    row = lax.broadcasted_iota(jnp.int32, (height, rows), 0)
    found = [one_hot(row == jnp.where(rank // 8 == index, goal * 8 + rank % 8, -1)) for index in range(slots.full)]
    if slots.half:
        late = rank - slots.full * 8
        found += [one_hot(row == jnp.where(late >= 0, goal * 8 + side * 4 + late, -1)) for side in range(2)]
    return found


def digits(slots, table_rows, placed):
    number = upright(placed % table_rows + 1)
    lane = lax.broadcasted_iota(jnp.int32, (number.shape[0], 2 * slots.groups), 1)
    digit = jnp.where(lane % 2 == 0, number // 128, number % 128)
    kept = [jnp.where(lane // 2 == index, digit, 0) for index in range(slots.groups)]
    return [value.astype(jnp.float32).astype(jnp.bfloat16) for value in kept]


def put(slots, found, table, out_ref, ids=None, base_ref=None):
    table = table.astype(jnp.bfloat16)

    def write(start, values):
        values, span = values.astype(jnp.bfloat16), slice(start, start + values.shape[1])
        out_ref[:, span] = values if base_ref is None else values + base_ref[:, span]

    for index in range(slots.full):
        write(index * slots.width, pick(found[index], table))
    if slots.half:
        left, right = (pick(found[slots.full + i], table[:, i * slots.half : (i + 1) * slots.half]) for i in range(2))
        write(slots.at, left + right)
    if ids is not None:
        pairs = [(found[index], ids[min(index, slots.full)]) for index in range(len(found))]
        write(slots.ids, sum(pick(select, digit) for select, digit in pairs))


def called(body, shapes, *operands):
    return pl.pallas_call(body, out_shape=shapes, compiler_params=LIMIT, cost_estimate=LIGHT)(*operands)


def exchanged(rows, devices):
    apart = rows.reshape(devices, 8, rows.shape[1])
    return lax.all_to_all(apart, BOTH, split_axis=0, concat_axis=0).reshape(rows.shape)


def halves(slots, pb, count):
    row = lax.broadcasted_iota(jnp.int32, (count, slots.width), 0)
    unit = lax.broadcasted_iota(jnp.int32, (count, slots.width), 1) // (slots.width // 4)
    peer = row // 8
    y, x, layer = peer // 2 % 2, peer % 2, peer // pb // 2 % 2
    apart = (unit // 2 != (x + y) % 2) & (unit % 2 != layer)
    return (y == 0) != apart


def added(slots, totals, hot, ref, index, lower):
    if index < slots.full:
        values = ref[:, index * slots.width : (index + 1) * slots.width]
    else:
        half = ref[:, slots.at : slots.at + slots.half]
        row = lax.broadcasted_iota(jnp.int32, (half.shape[0], slots.width), 0)
        lane = lax.broadcasted_iota(jnp.int32, (half.shape[0], slots.width), 1)
        values = jnp.where((row % 8 < 4) == (lane < slots.half), jnp.concatenate([half, half], axis=1), 0)
    values = [values] if lower is None else [jnp.where(lower, values, 0), jnp.where(lower, 0, values)]
    parts = [lax.dot_general(hot, v, TN, preferred_element_type=jnp.float32) for v in values]
    return parts if totals is None else [t + p for t, p in zip(totals, parts)]


def first_table_kernel(slots, pb, table_rows, split, got_ref, out_ref, hot_ref=None):
    count = got_ref.shape[0]
    lower = halves(slots, pb, count) if split else None
    entry = lax.broadcasted_iota(jnp.int32, (count, table_rows), 1)
    totals = None
    for index in range(slots.groups):
        at = slots.ids + 2 * index
        number = got_ref[:, at : at + 2].astype(jnp.float32)
        hot = one_hot(entry == (number[:, 0:1] * 128.0 + number[:, 1:2]).astype(jnp.int32) - 1)
        if hot_ref is not None:
            hot_ref[index] = hot
        totals = added(slots, totals, hot, got_ref, index, lower)
    for side, total in enumerate(totals):
        out_ref[:, side * slots.width : (side + 1) * slots.width] = total


def last_table_kernel(slots, pb, first_ref, hot_ref, got_ref, out_ref):
    width, half = slots.width, slots.width // 2
    upper = jnp.logical_not(halves(slots, pb, got_ref.shape[0]))
    totals = None
    for index in range(slots.groups):
        totals = added(slots, totals, hot_ref[index], got_ref, index, upper)
    out_ref[:, :width] = first_ref[:, :width] + totals[0]
    above = first_ref[:, width:] + totals[1]
    out_ref[:, width : width + half] = above[:, half:]
    out_ref[:, width + half :] = above[:, :half]


def on_device(train, query, residual, example_source, source_place):
    rows, depth = train.shape
    block = query.shape[0]
    ex, pb = lax.axis_size("ex"), lax.axis_size("pb")
    me_ex, me_pb = lax.axis_index("ex"), lax.axis_index("pb")
    devices = ex * pb
    table_rows = source_place.shape[0] // devices
    capacity = max(1, -(-2 * rows // devices))
    core, layer = me_ex % 2, (me_ex // 2) % 2
    deep = depth // 2
    on_core = lambda i: i ^ 1
    on_z = lambda i: i ^ 2
    on_x = lambda i: i ^ 1
    on_y = lambda i: i ^ 2
    whole = jax.ShapeDtypeStruct((table_rows, block * pb), jnp.float32)

    placed = jnp.take(source_place, example_source)
    packed_rows = lambda slots: jax.ShapeDtypeStruct((devices * 8, slots.lanes), jnp.bfloat16)

    if pb != 4 or ex % 4 != 0:
        other = moved(lax.dynamic_slice(train, (0, (1 - core) * deep), (rows, deep)), "ex", on_core)
        own = lax.dynamic_slice(train, (0, core * deep), (rows, deep))
        queries = lax.all_gather(lax.dynamic_slice(query, (0, core * deep), (block, deep)), "pb", tiled=True)
        slots = Slots(capacity, block * pb, True)
        own, other = scored([[own], [other]], [queries])

        def pack(scale, row, own_ref, got_ref, out_ref):
            found = selects(slots, table_rows, devices * 8, row)
            put(slots, found, weighted(own_ref, got_ref, scale), out_ref, digits(slots, table_rows, row))

        got = exchanged(packing(pack, packed_rows(slots), residual, placed, own, moved(other, "ex", on_core)), devices)
        return called(functools.partial(first_table_kernel, slots, pb, table_rows, False), whole, got)

    half = block // 2
    lent = half // 2 // 16 * 16
    ends = half - lent
    front, back, front_end, back_end, *others = cut_inputs(query, train, lent, 4)
    x_one = moved(front, "pb", on_x)
    y_one = moved(back, "pb", on_y)
    x_end = moved(back_end, "pb", on_x)
    y_end = moved(front_end, "pb", on_y)

    early, late = Slots(capacity, 2 * block, True), Slots(capacity, 2 * block, False)

    def units():
        me, layer = lax.axis_index("pb"), lax.axis_index("ex") // 2 % 2
        same = (me % 2 + me // 2) % 2
        unit = lambda near, part: (2 * (same if near else 1 - same) + part) * half
        return unit, layer, 1 - layer

    def first_pack(scale, row, home_ref, own_ref, got_ref, out_ref, base_ref):
        unit, mine, theirs = units()
        found = selects(early, table_rows, devices * 8, row)
        near = weighted(own_ref, got_ref, scale)
        table = ordered(early, weighted(home_ref, None, scale), [(unit(True, 0), block)])
        table += ordered(early, near, [(unit(False, mine), half), (unit(False, theirs), half)])
        put(early, found, table, out_ref, digits(early, table_rows, row))
        left = [(None, 2 * half), (unit(False, theirs) + lent, ends), (unit(False, mine) + lent, ends)]
        put(late, found, ordered(late, near, left), base_ref)

    def last_pack(scale, row, own_z, got_z, own_ref, got_ref, base_ref, out_ref):
        unit, mine, theirs = units()
        found = selects(late, table_rows, devices * 8, row)
        lent_spans = [(unit(False, theirs), lent), (unit(False, mine), lent)]
        spans = [(unit(True, theirs), half), (unit(True, mine), half)]
        table = ordered(late, weighted(own_z, got_z, scale), lent_spans)
        put(late, found, table + ordered(late, weighted(own_ref, got_ref, scale), spans), out_ref, None, base_ref)

    others = [moved(part, "ex", on_core) for part in others]
    own = lax.dynamic_slice(train, (0, core * deep), (rows, deep))
    (scores_own,) = scored([[train]], [query])
    x_one, y_one, others, own, scores_own, placed = lax.optimization_barrier(
        (x_one, y_one, others, own, scores_own, placed)
    )

    (z_sent,) = stacked([(x_one, 0, lent), (y_one, 0, lent)])
    z_lent = moved(z_sent, "ex", on_z)
    x_two = moved(y_one, "pb", on_x)
    y_two = moved(x_one, "pb", on_y)

    own_a, other_a = scored([[own], others], [x_one, y_one, x_end, y_end])
    got_a = moved(other_a, "ex", on_core)
    shapes = [packed_rows(early), packed_rows(late)]
    rows_a, base = packing(first_pack, shapes, residual, placed, scores_own, own_a, got_a)
    sent_a = exchanged(rows_a, devices)
    own, others, base = lax.optimization_barrier((own, others, base))

    own_z, other_z = scored([[own], others], [z_lent])
    x_two, y_two, own_z, other_z = lax.optimization_barrier((x_two, y_two, own_z, other_z))
    got_z = moved(other_z, "ex", on_core)
    pieces = [x_two, y_two]
    (other_b,) = scored([others], pieces)
    got_b = moved(other_b, "ex", on_core)
    (own_b,) = scored([[own]], pieces)
    sent_b = exchanged(packing(last_pack, packed_rows(late), residual, placed, own_z, got_z, own_b, got_b, base), devices)

    hot = jax.ShapeDtypeStruct((early.groups, devices * 8, table_rows), jnp.bfloat16)
    table, hot = called(functools.partial(first_table_kernel, early, pb, table_rows, True), [whole, hot], sent_a)
    return called(functools.partial(last_table_kernel, late, pb), whole, table, hot, sent_b)


def solution(mesh):
    return jax.shard_map(
        on_device,
        mesh=mesh,
        in_specs=(P(BOTH, None), P("pb", None), P(BOTH), P(BOTH), P()),
        out_specs=P(BOTH, None),
        check_vma=False,
    )
```

```python
import functools

import jax
import jax.numpy as jnp
from jax import lax
from jax.experimental import pallas as pl
from jax.experimental.pallas import tpu as pltpu
from jax.sharding import PartitionSpec as P

BOTH = ("ex", "pb")
NT = (((1,), (1,)), ((), ()))
LIMIT = pltpu.CompilerParams(vmem_limit_bytes=20 << 20)
LIGHT = pl.CostEstimate(flops=1, bytes_accessed=1, transcendentals=0)
HBM = pl.BlockSpec(memory_space=pltpu.HBM)
VMEM = pl.BlockSpec(memory_space=pltpu.VMEM)


def moved(value, target):
    ex, pb = lax.axis_size("ex"), lax.axis_size("pb")
    place = lambda e, p: e * pb + p
    return lax.ppermute(value, BOTH, [(place(e, p), place(*target(e, p))) for e in range(ex) for p in range(pb)])


def one_hot(hits):
    return jnp.where(hits, 1.0, 0.0).astype(jnp.bfloat16)


def pick(select, values):
    return jnp.dot(select, values, preferred_element_type=jnp.float32)


def scores_kernel(groups, count, *refs):
    held = sum(groups)
    rows, pieces, outs = refs[:held], refs[held : held + count], refs[held + count :]
    stack = lambda arrays: arrays[0][...] if len(arrays) == 1 else jnp.concatenate([a[...] for a in arrays], axis=0)
    total = lax.dot_general(stack(rows), stack(pieces), NT, preferred_element_type=jnp.float32)
    at = 0
    for out in outs:
        part = total[at : at + out.shape[0]]
        at += out.shape[0]

        @pl.when(pl.program_id(0) == 0)
        def _():
            out[...] = part

        @pl.when(pl.program_id(0) > 0)
        def _():
            out[...] += part


def scored(groups, pieces):
    width, deep = sum(piece.shape[0] for piece in pieces), pieces[0].shape[1]
    arrays = [rows for group in groups for rows in group]
    shapes = [jax.ShapeDtypeStruct((sum(rows.shape[0] for rows in group), width), jnp.float32) for group in groups]
    steps = 2
    chunk = lambda array: pl.BlockSpec((array.shape[0], deep // steps), lambda k: (0, k))
    return pl.pallas_call(
        functools.partial(scores_kernel, [len(group) for group in groups], len(pieces)),
        grid=(steps,),
        in_specs=[chunk(array) for array in [*arrays, *pieces]],
        out_specs=[pl.BlockSpec(shape.shape, lambda k: (0, 0)) for shape in shapes],
        out_shape=shapes,
        compiler_params=LIMIT,
        cost_estimate=LIGHT,
    )(*arrays, *pieces)


def copied(query, count):
    depth = query.shape[1]
    parts = 4
    height = count // parts

    def body(query_ref, out_ref, held, sems):
        mine = (lax.axis_index("ex") // 2 + lax.axis_index("ex")) % 2
        start = mine * (query_ref.shape[0] // 2)
        spans = [pl.ds(part * height, height) for part in range(parts)]
        source = lambda part: query_ref.at[pl.ds(pl.multiple_of(start + part * height, 16), height)]
        arriving = [pltpu.make_async_copy(source(i), held.at[spans[i]], sems.at[i]) for i in range(parts)]
        leaving = [pltpu.make_async_copy(held.at[spans[i]], out_ref.at[spans[i]], sems.at[parts + i]) for i in range(parts)]
        for copy in arriving:
            copy.start()
        for first, second in zip(arriving, leaving):
            first.wait()
            second.start()
        for copy in leaving:
            copy.wait()

    return pl.pallas_call(
        body,
        in_specs=[HBM],
        out_specs=HBM,
        out_shape=jax.ShapeDtypeStruct((count, depth), query.dtype),
        scratch_shapes=[pltpu.VMEM((count, depth), query.dtype), pltpu.SemaphoreType.DMA((2 * parts,))],
        compiler_params=pltpu.CompilerParams(vmem_limit_bytes=60 << 20),
        cost_estimate=LIGHT,
    )(query)


class Slots:
    def __init__(self, capacity, width, ids):
        self.width = width
        self.full, rest = capacity // 8, capacity % 8
        if rest > 4:
            self.full, rest = self.full + 1, 0
        self.half = width // 2 if rest else 0
        self.groups = self.full + (1 if rest else 0)
        self.at = self.full * width
        self.ids = self.at + self.half
        self.lanes = self.ids + (2 * self.groups if ids else 0)


def ordered(slots, scores, spans):
    column = jnp.concatenate(
        [
            jnp.full((count, 1), -1, jnp.int32)
            if base is None
            else lax.broadcasted_iota(jnp.int32, (count, 1), 0) + base
            for base, count in spans
        ],
        axis=0,
    )
    place = lax.broadcasted_iota(jnp.int32, (column.shape[0], slots.width), 1)
    return pick(scores, one_hot(place == column))


def upright(row):
    count = row.shape[1]
    diagonal = lax.broadcasted_iota(jnp.int32, (count, count), 0) == lax.broadcasted_iota(jnp.int32, (count, count), 1)
    return jnp.sum(jnp.where(diagonal, row, jnp.zeros_like(row)), axis=1, keepdims=True)


def flat(column):
    count = column.shape[0]
    diagonal = lax.broadcasted_iota(jnp.int32, (count, count), 0) == lax.broadcasted_iota(jnp.int32, (count, count), 1)
    return jnp.sum(jnp.where(diagonal, column, jnp.zeros_like(column)), axis=0, keepdims=True)


def packing(body, shape, residual, placed, *operands):
    rows = residual.shape[0]

    def kernel(scale_ref, row_ref, *refs):
        *refs, scale, row, sems = refs
        copies = [pltpu.make_async_copy(scale_ref, scale, sems.at[0]), pltpu.make_async_copy(row_ref, row, sems.at[1])]
        for copy in copies:
            copy.start()
        for copy in copies:
            copy.wait()
        body(scale[...], row[...], *refs)

    return pl.pallas_call(
        kernel,
        in_specs=[HBM] * 2 + [VMEM] * len(operands),
        out_shape=shape,
        scratch_shapes=[
            pltpu.VMEM((1, rows), residual.dtype),
            pltpu.VMEM((1, rows), placed.dtype),
            pltpu.SemaphoreType.DMA((2,)),
        ],
        compiler_params=LIMIT,
        cost_estimate=LIGHT,
    )(residual[None, :], placed[None, :], *operands)


def weighted(own, got, scale):
    return ((own[...] if got is None else own[...] + got[...]) * upright(scale)).astype(jnp.bfloat16)


def selects(slots, table_rows, height, placed):
    rows = placed.shape[1]
    goal = placed // table_rows
    same = upright(goal) == goal
    before = lax.broadcasted_iota(jnp.int32, (rows, 1), 0) < lax.broadcasted_iota(jnp.int32, (1, rows), 1)
    rank = jnp.sum(jnp.where(same & before, 1, 0), axis=0, keepdims=True)
    targets = [jnp.where(rank // 8 == index, goal * 8 + rank % 8, -1) for index in range(slots.full)]
    if slots.half:
        late = rank - slots.full * 8
        sides = [jnp.where(late >= 0, goal * 8 + side * 4 + late, -1) for side in range(2)]
        targets.append(jnp.concatenate(sides, axis=1))
    row = lambda target: lax.broadcasted_iota(jnp.int32, (height, target.shape[1]), 0)
    return [one_hot(row(target) == target) for target in targets]


def digits(slots, table_rows, placed):
    number = upright(placed % table_rows + 1)
    lane = lax.broadcasted_iota(jnp.int32, (number.shape[0], 2 * slots.groups), 1)
    digit = jnp.where(lane % 2 == 0, number // 128, number % 128)
    kept = [jnp.where(lane // 2 == index, digit, 0) for index in range(slots.groups)]
    return [value.astype(jnp.float32).astype(jnp.bfloat16) for value in kept]


def put(slots, found, table, out_ref, ids=None, base_ref=None):
    table = table.astype(jnp.bfloat16)

    def write(start, values):
        values, span = values.astype(jnp.bfloat16), slice(start, start + values.shape[1])
        out_ref[:, span] = values if base_ref is None else values + base_ref[:, span]

    for index in range(slots.full):
        write(index * slots.width, pick(found[index], table))
    stacked_halves = lambda left, right: jnp.concatenate([left, right], axis=0)
    if slots.half:
        write(slots.at, pick(found[slots.full], stacked_halves(table[:, : slots.half], table[:, slots.half :])))
    if ids is not None:
        digit = [ids[index] if index < slots.full else stacked_halves(ids[index], ids[index]) for index in range(len(found))]
        write(slots.ids, sum(pick(select, values) for select, values in zip(found, digit)))


def called(body, shapes, *operands):
    return pl.pallas_call(body, out_shape=shapes, compiler_params=LIMIT, cost_estimate=LIGHT)(*operands)


def exchanged(rows, devices):
    apart = rows.reshape(devices, 8, rows.shape[1])
    return lax.all_to_all(apart, BOTH, split_axis=0, concat_axis=0).reshape(rows.shape)


def halves(slots, pb, count):
    peer = lax.broadcasted_iota(jnp.int32, (count, 1), 0) // 8
    unit = lax.broadcasted_iota(jnp.int32, (1, slots.width), 1) // (slots.width // 4)
    y, x, layer = peer // 2 % 2, peer % 2, peer // pb // 2 % 2
    apart = (unit // 2 != (x + y) % 2) & (unit % 2 != layer)
    return (y == 0) != apart


def added(slots, totals, hot, ref, index, lower):
    if index < slots.full:
        values = ref[:, index * slots.width : (index + 1) * slots.width]
    else:
        half = ref[:, slots.at : slots.at + slots.half]
        row = lax.broadcasted_iota(jnp.int32, (half.shape[0], 1), 0)
        lane = lax.broadcasted_iota(jnp.int32, (1, slots.width), 1)
        values = jnp.where((row % 8 < 4) == (lane < slots.half), jnp.concatenate([half, half], axis=1), 0)
    values = [values] if lower is None else [jnp.where(lower, values, 0), jnp.where(lower, 0, values)]
    parts = [pick(hot, v) for v in values]
    return parts if totals is None else [t + p for t, p in zip(totals, parts)]


def first_table_kernel(slots, pb, table_rows, split, got_ref, out_ref, hot_ref=None):
    count = got_ref.shape[0]
    lower = halves(slots, pb, count) if split else None
    entry = lax.broadcasted_iota(jnp.int32, (table_rows, count), 0)
    totals = None
    for index in range(slots.groups):
        at = slots.ids + 2 * index
        number = got_ref[:, at : at + 2].astype(jnp.float32)
        hot = one_hot(entry == flat(number[:, 0:1] * 128.0 + number[:, 1:2]).astype(jnp.int32) - 1)
        if hot_ref is not None:
            hot_ref[index] = hot
        totals = added(slots, totals, hot, got_ref, index, lower)
    for side, total in enumerate(totals):
        out_ref[:, side * slots.width : (side + 1) * slots.width] = total


def last_table_kernel(slots, pb, first_ref, hot_ref, got_ref, out_ref):
    width, half = slots.width, slots.width // 2
    upper = jnp.logical_not(halves(slots, pb, got_ref.shape[0]))
    totals = None
    for index in range(slots.groups):
        totals = added(slots, totals, hot_ref[index], got_ref, index, upper)
    out_ref[:, :width] = first_ref[:, :width] + totals[0]
    above = first_ref[:, width:] + totals[1]
    out_ref[:, width : width + half] = above[:, half:]
    out_ref[:, width + half :] = above[:, :half]


def on_device(train, query, residual, example_source, source_place):
    rows, depth = train.shape
    block = query.shape[0]
    ex, pb = lax.axis_size("ex"), lax.axis_size("pb")
    me_ex, me_pb = lax.axis_index("ex"), lax.axis_index("pb")
    devices = ex * pb
    table_rows = source_place.shape[0] // devices
    capacity = max(1, -(-2 * rows // devices))
    core, layer = me_ex % 2, (me_ex // 2) % 2
    on_core = lambda e, p: (e ^ 1, p)
    on_z = lambda e, p: (e ^ 2, p)
    near = lambda e, p: (e, p ^ (1 + e % 2))
    across = lambda e, p: (e, p ^ (2 - e % 2))
    whole = jax.ShapeDtypeStruct((table_rows, block * pb), jnp.float32)

    placed = jnp.take(source_place, example_source)
    packed_rows = lambda slots: jax.ShapeDtypeStruct((devices * 8, slots.lanes), jnp.bfloat16)

    if pb != 4 or ex % 4 != 0:
        deep = depth // 2
        other = moved(lax.dynamic_slice(train, (0, (1 - core) * deep), (rows, deep)), on_core)
        own = lax.dynamic_slice(train, (0, core * deep), (rows, deep))
        queries = lax.all_gather(lax.dynamic_slice(query, (0, core * deep), (block, deep)), "pb", tiled=True)
        slots = Slots(capacity, block * pb, True)
        own, other = scored([[own], [other]], [queries])

        def pack(scale, row, own_ref, got_ref, out_ref):
            found = selects(slots, table_rows, devices * 8, row)
            put(slots, found, weighted(own_ref, got_ref, scale), out_ref, digits(slots, table_rows, row))

        got = exchanged(packing(pack, packed_rows(slots), residual, placed, own, moved(other, on_core)), devices)
        return called(functools.partial(first_table_kernel, slots, pb, table_rows, False), whole, got)

    half = block // 2
    head = half * 2 // 3
    lent = head
    ends = half - lent
    mine = (layer + core) % 2
    cut = lambda start, count: lax.dynamic_slice(query, (start, 0), (count, depth))
    one = moved(copied(query, head), near)
    tail = moved(cut(mine * half + head, half - head), near)
    rest = moved(cut((1 - mine) * half + lent, ends), near)
    other = moved(train, on_core)

    early, late = Slots(capacity, 2 * block, True), Slots(capacity, 2 * block, False)

    def units():
        me = lax.axis_index("pb")
        same = (me % 2 + me // 2) % 2
        unit = lambda near, part: (2 * (same if near else 1 - same) + part) * half
        return unit, (lax.axis_index("ex") // 2 + lax.axis_index("ex")) % 2

    def first_pack(scale, row, home_ref, own_ref, got_ref, out_ref):
        unit, part = units()
        found = selects(early, table_rows, devices * 8, row)
        own, got = weighted(own_ref, None, scale), weighted(got_ref, None, scale)
        table = ordered(early, weighted(home_ref, None, scale), [(unit(True, 0), block)])
        table += ordered(early, own, [(unit(False, part), half)])
        table += ordered(early, got, [(unit(False, 1 - part), half)])
        put(early, found, table, out_ref, digits(early, table_rows, row))

    def last_pack(scale, row, own_ref, got_ref, out_ref):
        unit, part = units()
        found = selects(late, table_rows, devices * 8, row)

        def spans(side):
            across, beside = unit(True, side), unit(False, 1 - side)
            return [(beside, lent), (across, head), (across + head, half - head), (beside + lent, ends)]

        table = ordered(late, weighted(own_ref, None, scale), spans(part))
        table += ordered(late, weighted(got_ref, None, scale), spans(1 - part))
        put(late, found, table, out_ref)

    (scores_own,) = scored([[train]], [query])
    one, other, scores_own, placed = lax.optimization_barrier((one, other, scores_own, placed))
    z_lent = moved(one, on_z)
    two = moved(one, across)
    two_tail = moved(tail, across)

    own_a, other_a = scored([[train], [other]], [one, tail])
    got_a = moved(other_a, on_core)
    rows_a = packing(first_pack, packed_rows(early), residual, placed, scores_own, own_a, got_a)
    train, other, rows_a = lax.optimization_barrier((train, other, rows_a))
    sent_a = exchanged(rows_a, devices)

    pieces = [z_lent, two, two_tail, rest]
    own_b, other_b = scored([[train], [other]], pieces)
    got_b = moved(other_b, on_core)
    rows_b = packing(last_pack, packed_rows(late), residual, placed, own_b, got_b)
    sent_b = exchanged(rows_b, devices)

    hot = jax.ShapeDtypeStruct((early.groups, table_rows, devices * 8), jnp.bfloat16)
    table, hot = called(functools.partial(first_table_kernel, early, pb, table_rows, True), [whole, hot], sent_a)
    return called(functools.partial(last_table_kernel, late, pb), whole, table, hot, sent_b)


def solution(mesh):
    return jax.shard_map(
        on_device,
        mesh=mesh,
        in_specs=(P(BOTH, None), P("pb", None), P(BOTH), P(BOTH), P()),
        out_specs=P(BOTH, None),
        check_vma=False,
    )
```

```python
import functools

import jax
import jax.numpy as jnp
from jax import lax
from jax.experimental import pallas as pl
from jax.experimental.pallas import tpu as pltpu
from jax.sharding import PartitionSpec as P

BOTH = ("ex", "pb")
NT = (((1,), (1,)), ((), ()))
LIMIT = pltpu.CompilerParams(vmem_limit_bytes=14 << 20)
LIGHT = pl.CostEstimate(flops=1, bytes_accessed=1, transcendentals=0)
HBM = pl.BlockSpec(memory_space=pltpu.HBM)
VMEM = pl.BlockSpec(memory_space=pltpu.VMEM)


def moved(value, target):
    ex, pb = lax.axis_size("ex"), lax.axis_size("pb")
    place = lambda e, p: e * pb + p
    return lax.ppermute(value, BOTH, [(place(e, p), place(*target(e, p))) for e in range(ex) for p in range(pb)])


def one_hot(hits):
    return jnp.where(hits, 1.0, 0.0).astype(jnp.bfloat16)


def pick(select, values):
    return jnp.dot(select, values, preferred_element_type=jnp.float32)


def scores_kernel(groups, count, *refs):
    held = sum(groups)
    rows, pieces, outs = refs[:held], refs[held : held + count], refs[held + count :]
    stack = lambda arrays: arrays[0][...] if len(arrays) == 1 else jnp.concatenate([a[...] for a in arrays], axis=0)
    total = lax.dot_general(stack(rows), stack(pieces), NT, preferred_element_type=jnp.float32)
    at = 0
    for out in outs:
        part = total[at : at + out.shape[0]]
        at += out.shape[0]

        @pl.when(pl.program_id(0) == 0)
        def _():
            out[...] = part

        @pl.when(pl.program_id(0) > 0)
        def _():
            out[...] += part


def scored(groups, pieces):
    width, deep = sum(piece.shape[0] for piece in pieces), pieces[0].shape[1]
    arrays = [rows for group in groups for rows in group]
    shapes = [jax.ShapeDtypeStruct((sum(rows.shape[0] for rows in group), width), jnp.float32) for group in groups]
    steps = 2
    chunk = lambda array: pl.BlockSpec((array.shape[0], deep // steps), lambda k: (0, k))
    return pl.pallas_call(
        functools.partial(scores_kernel, [len(group) for group in groups], len(pieces)),
        grid=(steps,),
        in_specs=[chunk(array) for array in [*arrays, *pieces]],
        out_specs=[pl.BlockSpec(shape.shape, lambda k: (0, 0)) for shape in shapes],
        out_shape=shapes,
        compiler_params=LIMIT,
        cost_estimate=LIGHT,
    )(*arrays, *pieces)


def copied(query, count):
    depth = query.shape[1]
    parts = 2
    height = count // parts

    def body(query_ref, out_ref, held, sems):
        mine = (lax.axis_index("ex") // 2 + lax.axis_index("ex")) % 2
        start = mine * (query_ref.shape[0] // 2)
        spans = [pl.ds(part * height, height) for part in range(parts)]
        source = lambda part: query_ref.at[pl.ds(pl.multiple_of(start + part * height, 16), height)]
        arriving = [pltpu.make_async_copy(source(i), held.at[spans[i]], sems.at[i]) for i in range(parts)]
        leaving = [pltpu.make_async_copy(held.at[spans[i]], out_ref.at[spans[i]], sems.at[parts + i]) for i in range(parts)]
        for copy in arriving:
            copy.start()
        for first, second in zip(arriving, leaving):
            first.wait()
            second.start()
        for copy in leaving:
            copy.wait()

    return pl.pallas_call(
        body,
        in_specs=[HBM],
        out_specs=HBM,
        out_shape=jax.ShapeDtypeStruct((count, depth), query.dtype),
        scratch_shapes=[pltpu.VMEM((count, depth), query.dtype), pltpu.SemaphoreType.DMA((2 * parts,))],
        compiler_params=pltpu.CompilerParams(vmem_limit_bytes=60 << 20),
        cost_estimate=LIGHT,
    )(query)


class Slots:
    def __init__(self, capacity, width, ids):
        self.width = width
        self.full, rest = capacity // 8, capacity % 8
        if rest > 4:
            self.full, rest = self.full + 1, 0
        self.half = width // 2 if rest else 0
        self.groups = self.full + (1 if rest else 0)
        self.at = self.full * width
        self.ids = self.at + self.half
        self.lanes = self.ids + (2 * self.groups if ids else 0)


def ordered(slots, scores, spans):
    column = jnp.concatenate(
        [
            jnp.full((count, 1), -1, jnp.int32)
            if base is None
            else lax.broadcasted_iota(jnp.int32, (count, 1), 0) + base
            for base, count in spans
        ],
        axis=0,
    )
    place = lax.broadcasted_iota(jnp.int32, (column.shape[0], slots.width), 1)
    return pick(scores, one_hot(place == column))


def upright(row):
    count = row.shape[1]
    diagonal = lax.broadcasted_iota(jnp.int32, (count, count), 0) == lax.broadcasted_iota(jnp.int32, (count, count), 1)
    return jnp.sum(jnp.where(diagonal, row, jnp.zeros_like(row)), axis=1, keepdims=True)


def flat(column):
    count = column.shape[0]
    diagonal = lax.broadcasted_iota(jnp.int32, (count, count), 0) == lax.broadcasted_iota(jnp.int32, (count, count), 1)
    return jnp.sum(jnp.where(diagonal, column, jnp.zeros_like(column)), axis=0, keepdims=True)


def packing(body, shape, residual, placed, *operands):
    rows = residual.shape[0]

    def kernel(scale_ref, row_ref, *refs):
        *refs, scale, row, sems = refs
        copies = [pltpu.make_async_copy(scale_ref, scale, sems.at[0]), pltpu.make_async_copy(row_ref, row, sems.at[1])]
        for copy in copies:
            copy.start()
        for copy in copies:
            copy.wait()
        body(scale[...], row[...], *refs)

    return pl.pallas_call(
        kernel,
        in_specs=[HBM] * 2 + [VMEM] * len(operands),
        out_shape=shape,
        scratch_shapes=[
            pltpu.VMEM((1, rows), residual.dtype),
            pltpu.VMEM((1, rows), placed.dtype),
            pltpu.SemaphoreType.DMA((2,)),
        ],
        compiler_params=LIMIT,
        cost_estimate=LIGHT,
    )(residual[None, :], placed[None, :], *operands)


def weighted(own, got, scale):
    return ((own[...] if got is None else own[...] + got[...]) * upright(scale)).astype(jnp.bfloat16)


def selects(slots, table_rows, height, placed):
    rows = placed.shape[1]
    goal = placed // table_rows
    same = upright(goal) == goal
    before = lax.broadcasted_iota(jnp.int32, (rows, 1), 0) < lax.broadcasted_iota(jnp.int32, (1, rows), 1)
    rank = jnp.sum(jnp.where(same & before, 1, 0), axis=0, keepdims=True)
    targets = [jnp.where(rank // 8 == index, goal * 8 + rank % 8, -1) for index in range(slots.full)]
    if slots.half:
        late = rank - slots.full * 8
        sides = [jnp.where(late >= 0, goal * 8 + side * 4 + late, -1) for side in range(2)]
        targets.append(jnp.concatenate(sides, axis=1))
    row = lambda target: lax.broadcasted_iota(jnp.int32, (height, target.shape[1]), 0)
    return [one_hot(row(target) == target) for target in targets]


def digits(slots, table_rows, placed):
    number = upright(placed % table_rows + 1)
    lane = lax.broadcasted_iota(jnp.int32, (number.shape[0], 2 * slots.groups), 1)
    digit = jnp.where(lane % 2 == 0, number // 128, number % 128)
    kept = [jnp.where(lane // 2 == index, digit, 0) for index in range(slots.groups)]
    return [value.astype(jnp.float32).astype(jnp.bfloat16) for value in kept]


def put(slots, found, table, out_ref, ids=None, base_ref=None):
    table = table.astype(jnp.bfloat16)

    def write(start, values):
        values, span = values.astype(jnp.bfloat16), slice(start, start + values.shape[1])
        out_ref[:, span] = values if base_ref is None else values + base_ref[:, span]

    for index in range(slots.full):
        write(index * slots.width, pick(found[index], table))
    stacked_halves = lambda left, right: jnp.concatenate([left, right], axis=0)
    if slots.half:
        write(slots.at, pick(found[slots.full], stacked_halves(table[:, : slots.half], table[:, slots.half :])))
    if ids is not None:
        digit = [ids[index] if index < slots.full else stacked_halves(ids[index], ids[index]) for index in range(len(found))]
        write(slots.ids, sum(pick(select, values) for select, values in zip(found, digit)))


def called(body, shapes, *operands):
    return pl.pallas_call(body, out_shape=shapes, compiler_params=LIMIT, cost_estimate=LIGHT)(*operands)


def exchanged(rows, devices):
    apart = rows.reshape(devices, 8, rows.shape[1])
    return lax.all_to_all(apart, BOTH, split_axis=0, concat_axis=0).reshape(rows.shape)


def halves(slots, pb, count):
    peer = lax.broadcasted_iota(jnp.int32, (count, 1), 0) // 8
    unit = lax.broadcasted_iota(jnp.int32, (1, slots.width), 1) // (slots.width // 4)
    y, x, layer = peer // 2 % 2, peer % 2, peer // pb // 2 % 2
    apart = (unit // 2 != (x + y) % 2) & (unit % 2 != layer)
    return (y == 0) != apart


def added(slots, totals, hot, ref, index, lower):
    if index < slots.full:
        values = ref[:, index * slots.width : (index + 1) * slots.width]
    else:
        half = ref[:, slots.at : slots.at + slots.half]
        row = lax.broadcasted_iota(jnp.int32, (half.shape[0], 1), 0)
        lane = lax.broadcasted_iota(jnp.int32, (1, slots.width), 1)
        values = jnp.where((row % 8 < 4) == (lane < slots.half), jnp.concatenate([half, half], axis=1), 0)
    values = [values] if lower is None else [jnp.where(lower, values, 0), jnp.where(lower, 0, values)]
    parts = [pick(hot, v) for v in values]
    return parts if totals is None else [t + p for t, p in zip(totals, parts)]


def first_table_kernel(slots, pb, table_rows, split, got_ref, out_ref, hot_ref=None):
    count = got_ref.shape[0]
    lower = halves(slots, pb, count) if split else None
    entry = lax.broadcasted_iota(jnp.int32, (table_rows, count), 0)
    totals = None
    for index in range(slots.groups):
        at = slots.ids + 2 * index
        number = got_ref[:, at : at + 2].astype(jnp.float32)
        hot = one_hot(entry == flat(number[:, 0:1] * 128.0 + number[:, 1:2]).astype(jnp.int32) - 1)
        if hot_ref is not None:
            hot_ref[index] = hot
        totals = added(slots, totals, hot, got_ref, index, lower)
    for side, total in enumerate(totals):
        out_ref[:, side * slots.width : (side + 1) * slots.width] = total


def last_table_kernel(slots, pb, first_ref, hot_ref, got_ref, out_ref):
    width, half = slots.width, slots.width // 2
    upper = jnp.logical_not(halves(slots, pb, got_ref.shape[0]))
    totals = None
    for index in range(slots.groups):
        totals = added(slots, totals, hot_ref[index], got_ref, index, upper)
    out_ref[:, :width] = first_ref[:, :width] + totals[0]
    above = first_ref[:, width:] + totals[1]
    out_ref[:, width : width + half] = above[:, half:]
    out_ref[:, width + half :] = above[:, :half]


def on_device(train, query, residual, example_source, source_place):
    rows, depth = train.shape
    block = query.shape[0]
    ex, pb = lax.axis_size("ex"), lax.axis_size("pb")
    me_ex, me_pb = lax.axis_index("ex"), lax.axis_index("pb")
    devices = ex * pb
    table_rows = source_place.shape[0] // devices
    capacity = max(1, -(-2 * rows // devices))
    core, layer = me_ex % 2, (me_ex // 2) % 2
    on_core = lambda e, p: (e ^ 1, p)
    on_z = lambda e, p: (e ^ 2, p)
    near = lambda e, p: (e, p ^ (1 + e % 2))
    across = lambda e, p: (e, p ^ (2 - e % 2))
    whole = jax.ShapeDtypeStruct((table_rows, block * pb), jnp.float32)

    placed = jnp.take(source_place, example_source)
    packed_rows = lambda slots: jax.ShapeDtypeStruct((devices * 8, slots.lanes), jnp.bfloat16)

    if pb != 4 or ex % 4 != 0:
        deep = depth // 2
        other = moved(lax.dynamic_slice(train, (0, (1 - core) * deep), (rows, deep)), on_core)
        own = lax.dynamic_slice(train, (0, core * deep), (rows, deep))
        queries = lax.all_gather(lax.dynamic_slice(query, (0, core * deep), (block, deep)), "pb", tiled=True)
        slots = Slots(capacity, block * pb, True)
        own, other = scored([[own], [other]], [queries])

        def pack(scale, row, own_ref, got_ref, out_ref):
            found = selects(slots, table_rows, devices * 8, row)
            put(slots, found, weighted(own_ref, got_ref, scale), out_ref, digits(slots, table_rows, row))

        got = exchanged(packing(pack, packed_rows(slots), residual, placed, own, moved(other, on_core)), devices)
        return called(functools.partial(first_table_kernel, slots, pb, table_rows, False), whole, got)

    half = block // 2
    head = half * 2 // 3
    lent = head
    ends = half - lent
    mine = (layer + core) % 2
    cut = lambda start, count: lax.dynamic_slice(query, (start, 0), (count, depth))
    one = moved(copied(query, head), near)
    tail = moved(cut(mine * half + head, half - head), near)
    rest = moved(cut((1 - mine) * half + lent, ends), near)
    other = moved(train, on_core)

    early, late = Slots(capacity, 2 * block, True), Slots(capacity, 2 * block, False)

    def units():
        me = lax.axis_index("pb")
        same = (me % 2 + me // 2) % 2
        unit = lambda near, part: (2 * (same if near else 1 - same) + part) * half
        return unit, (lax.axis_index("ex") // 2 + lax.axis_index("ex")) % 2

    def first_pack(scale, row, home_ref, own_ref, got_ref, out_ref):
        unit, part = units()
        found = selects(early, table_rows, devices * 8, row)
        own, got = weighted(own_ref, None, scale), weighted(got_ref, None, scale)
        table = ordered(early, weighted(home_ref, None, scale), [(unit(True, 0), block)])
        table += ordered(early, own, [(unit(False, part), half)])
        table += ordered(early, got, [(unit(False, 1 - part), half)])
        put(early, found, table, out_ref, digits(early, table_rows, row))

    def last_pack(scale, row, own_ref, got_ref, out_ref):
        unit, part = units()
        found = selects(late, table_rows, devices * 8, row)

        def spans(side):
            across, beside = unit(True, side), unit(False, 1 - side)
            return [(beside, lent), (across, head), (across + head, half - head), (beside + lent, ends)]

        table = ordered(late, weighted(own_ref, None, scale), spans(part))
        table += ordered(late, weighted(got_ref, None, scale), spans(1 - part))
        put(late, found, table, out_ref)

    (scores_own,) = scored([[train]], [query])
    one, other, scores_own, placed = lax.optimization_barrier((one, other, scores_own, placed))
    z_lent = moved(one, on_z)
    two = moved(one, across)
    two_tail = moved(tail, across)

    own_a, other_a = scored([[train], [other]], [one, tail])
    got_a = moved(other_a, on_core)
    rows_a = packing(first_pack, packed_rows(early), residual, placed, scores_own, own_a, got_a)
    train, other, rows_a = lax.optimization_barrier((train, other, rows_a))
    sent_a = exchanged(rows_a, devices)

    pieces = [z_lent, two, two_tail, rest]
    own_b, other_b = scored([[train], [other]], pieces)
    got_b = moved(other_b, on_core)
    rows_b = packing(last_pack, packed_rows(late), residual, placed, own_b, got_b)
    sent_b = exchanged(rows_b, devices)

    hot = jax.ShapeDtypeStruct((early.groups, table_rows, devices * 8), jnp.bfloat16)
    table, hot = called(functools.partial(first_table_kernel, early, pb, table_rows, True), [whole, hot], sent_a)
    return called(functools.partial(last_table_kernel, late, pb), whole, table, hot, sent_b)


def solution(mesh):
    return jax.shard_map(
        on_device,
        mesh=mesh,
        in_specs=(P(BOTH, None), P("pb", None), P(BOTH), P(BOTH), P()),
        out_specs=P(BOTH, None),
        check_vma=False,
    )
```
